128 devices in a mesh: row: 16 (over y_lo, z, core), col: 8 (over y_hi, x).
Axes of the slice: x: 4, y: 4 (y_hi: 2, y_lo: 2; y = y_hi * 2 + y_lo), z: 4, core: 2. Of those that a mesh axis runs over, the one named last changes fastest.
Arguments:
- grad_out: float32 [16, 512, 2048], P(None, 'row', 'col'), may hold values from -6 to 6
- input_spectrum: float32 [2, 16, 1024, 2048], P(None, None, ('row', 'col')), may hold values from -6 to 6
- filter_spectrum: float32 [2, 16, 1024, 2048], P(None, None, ('row', 'col')), may hold values from -6 to 6
Outputs:
- grad_input: float32 [16, 512, 2048], P(None, 'row', 'col')
- grad_filter: float32 [16, 512, 2048], P(None, 'row', 'col')
The draws below stay inside these ranges and needn't reach their ends.
All inputs are finite; a program needn't handle non-finite values.
Results may differ from the reference program's by a relative error of at most 0.00007.
Values sent between devices are 32-bit elements; how exact they have to be, the bound alone decides.
A program may use at most 192 MiB of HBM per device.

```python
import jax
import jax.numpy as jnp

N1 = 1024
N2 = 2048
CH = 16
HALF1 = 512


def block_scale(key, extent, shards, low, largest):
    level = 1.0
    for position, parts in shards:
        draws = jax.random.uniform(jax.random.fold_in(jax.random.fold_in(key, 6), position), (parts,), jnp.float32, low / len(shards), largest / len(shards))
        level = level * jnp.repeat(jnp.exp(draws), extent[position] // parts).reshape((-1,) + (1,) * (len(extent) - 1 - position))
    return level


def normal_values(stream_key, dims, deviation, reach, shards=(), kind=jnp.bfloat16):
    drawn = deviation * jax.random.normal(stream_key, dims, jnp.float32)
    if shards:
        drawn = drawn * block_scale(stream_key, dims, shards, -0.22, 0.18)
    return jnp.clip(drawn, -reach, reach).astype(kind)


def setup_inputs(seed: int = 0) -> dict:
    arg_keys = jax.random.split(jax.random.key(seed), 4)
    grad_out = normal_values(arg_keys[0], (CH, HALF1, N2), 1.0, 6.0, ((1, 16), (2, 8)), jnp.float32)
    input_spectrum = normal_values(arg_keys[1], (2, CH, N1, N2), 1.0, 6.0, ((2, 128),), jnp.float32)
    filter_spectrum = normal_values(arg_keys[2], (2, CH, N1, N2), 1.0, 6.0, ((2, 128),), jnp.float32)
    return {"grad_out": grad_out, "input_spectrum": input_spectrum, "filter_spectrum": filter_spectrum}


def reference(grad_out, input_spectrum, filter_spectrum):
    channels = grad_out.shape[0]
    total_len = N1 * N2
    length = HALF1 * N2
    flat = grad_out.reshape(channels, length)
    padded = jnp.concatenate([flat, jnp.zeros((channels, total_len - length), flat.dtype)], axis=1)
    upstream = jnp.fft.fft(padded, axis=1)

    def natural(spectrum):
        joined = spectrum[0] + 1j * spectrum[1]
        return jnp.transpose(joined, (0, 2, 1)).reshape(channels, total_len)

    def inverse(other):
        values = jnp.real(jnp.fft.ifft(upstream * jnp.conj(other), axis=1))
        return values[:, :length].reshape(channels, HALF1, N2).astype(grad_out.dtype)

    grad_input = inverse(natural(filter_spectrum))
    grad_filter = inverse(natural(input_spectrum))
    return grad_input, grad_filter
```

```python
import functools

import jax
import jax.numpy as jnp
import ml_dtypes
import numpy as np
from jax import lax
from jax.experimental import pallas as pl
from jax.experimental.pallas import tpu as pltpu
from jax.sharding import PartitionSpec as P

MESH = pl.DeviceIdType.MESH
F32 = jnp.float32
BF16 = jnp.bfloat16

ROWS, COLS = 16, 8
DEVS = ROWS * COLS
CH = 16
N1, N2 = 1024, 2048
HALF1 = N1 // 2
TOTAL = N1 * N2
K1L = N1 // DEVS
N1L = HALF1 // ROWS
B = N2 // COLS
RAD = 8
GROUPS, PER = 4, 4
ROOT_HALF = float(np.sqrt(0.5))


def split_table(table):
    table = np.asarray(table, np.float64)
    high = table.astype(np.float32).astype(ml_dtypes.bfloat16)
    low = (table - high.astype(np.float64)).astype(np.float32).astype(ml_dtypes.bfloat16)
    return np.stack([high, low])


@functools.lru_cache(None)
def tables():
    n1 = np.arange(HALF1)
    k1 = np.arange(N1)
    angle = 2 * np.pi * ((k1[:, None] * n1[None, :]) % N1) / N1
    first = np.stack([np.cos(angle), -np.sin(angle)]).reshape(2, DEVS, K1L, HALF1)
    first = first.transpose(1, 0, 2, 3).reshape(2 * N1, HALF1)
    last = (first.T / TOTAL).reshape(HALF1, ROWS, 2 * N1 // ROWS).transpose(1, 0, 2)
    b = np.arange(B)
    angle = 2 * np.pi * ((b[:, None] * b[None, :]) % B) / B
    c, s = np.cos(angle), np.sin(angle)
    inner = np.block([[c, -s], [s, c]])
    back = np.block([[c, s], [-s, c]])
    place = np.zeros((B, B))
    place[b, (b % RAD) * (B // RAD) + b // RAD] = 1
    return (
        split_table(first),
        split_table(last),
        np.concatenate([split_table(inner), split_table(back)]),
        place.astype(ml_dtypes.bfloat16),
    )


def split(value):
    high = value.astype(BF16)
    low = (value - high.astype(F32)).astype(BF16)
    return high, low


def mm(a, b):
    return jnp.dot(a, b, preferred_element_type=F32)


def mm3(ah, al, bh, bl):
    return mm(ah, bh) + (mm(ah, bl) + mm(al, bh))


def dft4(re, im, sign):
    p0r, p0i = re[0] + re[2], im[0] + im[2]
    p1r, p1i = re[0] - re[2], im[0] - im[2]
    r0r, r0i = re[1] + re[3], im[1] + im[3]
    r1r, r1i = re[1] - re[3], im[1] - im[3]
    out_r = [p0r + r0r, None, p0r - r0r, None]
    out_i = [p0i + r0i, None, p0i - r0i, None]
    if sign > 0:
        out_r[1], out_i[1] = p1r - r1i, p1i + r1r
        out_r[3], out_i[3] = p1r + r1i, p1i - r1r
    else:
        out_r[1], out_i[1] = p1r + r1i, p1i - r1r
        out_r[3], out_i[3] = p1r - r1i, p1i + r1r
    return out_r, out_i


def dft8(re, im, sign):
    ur = [re[a] + re[a + 4] for a in range(4)]
    ui = [im[a] + im[a + 4] for a in range(4)]
    vr = [re[a] - re[a + 4] for a in range(4)]
    vi = [im[a] - im[a + 4] for a in range(4)]
    even_r, even_i = dft4(ur, ui, sign)
    if sign > 0:
        v1 = ((vr[1] - vi[1]) * ROOT_HALF, (vi[1] + vr[1]) * ROOT_HALF)
        v2 = (-vi[2], vr[2])
        v3 = ((vr[3] + vi[3]) * -ROOT_HALF, (vr[3] - vi[3]) * ROOT_HALF)
    else:
        v1 = ((vr[1] + vi[1]) * ROOT_HALF, (vi[1] - vr[1]) * ROOT_HALF)
        v2 = (vi[2], -vr[2])
        v3 = ((vi[3] - vr[3]) * ROOT_HALF, (vr[3] + vi[3]) * -ROOT_HALF)
    odd_r, odd_i = dft4([vr[0], v1[0], v2[0], v3[0]], [vi[0], v1[1], v2[1], v3[1]], sign)
    out_r = [None] * 8
    out_i = [None] * 8
    for t in range(4):
        out_r[2 * t], out_i[2 * t] = even_r[t], even_i[t]
        out_r[2 * t + 1], out_i[2 * t + 1] = odd_r[t], odd_i[t]
    return out_r, out_i


def row_at(row, q, m, way):
    yl, z, core = lax.div(row, 8), lax.rem(lax.div(row, 2), 4), lax.rem(row, 2)
    dyl, dc, dz = lax.div(m, 2), lax.rem(m, 2), lax.rem(q + m, 4)
    dz = dz if way > 0 else 4 - dz
    return lax.rem(yl + dyl, 2) * 8 + lax.rem(z + dz, 4) * 2 + lax.rem(core + dc, 2)


def col_at(col, i):
    yh, x = lax.div(col, 4), lax.rem(col, 4)
    return lax.rem(yh + lax.div(i, 4), 2) * 4 + lax.rem(x + lax.rem(i, 4), 4)


def loop(lower, upper, body):
    def step(i, carry):
        body(i)
        return carry

    lax.fori_loop(lower, upper, step, 0)


def kernel(
    grad_ref, sx_ref, sh_ref, first_ref, last_ref, inner_ref, place_ref,
    oh_ref, ox_ref,
    raw, spec, first, last, inner, place, xg, xs, bsend, brecv, va, vt,
    ah, al, us, vs, tsend, trecv, acc,
    lsem, s1, r1, s2, r2, s4, r4, s5, r5,
):
    row = lax.axis_index("row")
    col = lax.axis_index("col")
    me = row * COLS + col

    barrier = pltpu.get_barrier_semaphore()

    def greet(i):
        d = lax.rem(me + i, DEVS)
        pl.semaphore_signal(
            barrier, inc=1, device_id=(lax.div(d, COLS), lax.rem(d, COLS)), device_id_type=MESH
        )

    loop(1, DEVS, greet)

    loads = [
        pltpu.make_async_copy(sh_ref, raw.at[0], lsem.at[0]),
        pltpu.make_async_copy(sx_ref, raw.at[1], lsem.at[1]),
        pltpu.make_async_copy(place_ref, place, lsem.at[2]),
        pltpu.make_async_copy(first_ref, first, lsem.at[3]),
        pltpu.make_async_copy(inner_ref, inner, lsem.at[4]),
        pltpu.make_async_copy(last_ref, last, lsem.at[5]),
    ]
    for load in loads:
        load.start()

    k1 = me * K1L + lax.broadcasted_iota(jnp.int32, (K1L, B), 0)
    lane = lax.broadcasted_iota(jnp.int32, (K1L, B), 1)

    def turn(a):
        phase = lax.rem(k1 * a, TOTAL // B)
        phase = jnp.where(phase > TOTAL // B // 2, phase - TOTAL // B, phase)
        angle = phase.astype(F32) * (2.0 * np.pi * B / TOTAL)
        va[0, a] = jnp.cos(angle)
        va[1, a] = jnp.sin(angle)
        phase = lane * (k1 + N1 * a)
        phase = jnp.where(phase > TOTAL // 2, phase - TOTAL, phase)
        angle = phase.astype(F32) * (2.0 * np.pi / TOTAL)
        vt[0, a] = jnp.cos(angle)
        vt[1, a] = jnp.sin(angle)

    loop(0, RAD, turn)

    pl.semaphore_wait(barrier, DEVS - 1)

    own_rows = pl.ds(pl.multiple_of(row * N1L, N1L), N1L)
    own_x = pltpu.make_async_copy(grad_ref.at[row], xg.at[own_rows], r1)
    own_x.start()

    def send_x(i):
        r = lax.rem(row + i, ROWS)
        pltpu.make_async_remote_copy(
            src_ref=grad_ref.at[r], dst_ref=xg.at[own_rows], send_sem=s1, recv_sem=r1,
            device_id=(r, col), device_id_type=MESH,
        ).start()

    loop(1, ROWS, send_x)

    for load in loads[:3]:
        load.wait()
    lane128 = lax.broadcasted_iota(jnp.int32, (16, 128), 1)

    def order(n):
        which, part, c0 = lax.div(n, 8), lax.rem(lax.div(n, 4), 2), lax.rem(n, 4) * 4
        blocks = []
        for c in range(4):
            whole = raw[which, part, c0 + c]
            blocks += [whole[:, j * B : (j + 1) * B] for j in range(RAD)]
        high, low = split(jnp.concatenate(blocks, axis=0))
        placed = mm(high, place[...]) + mm(low, place[...])
        for c in range(4):
            for h in range(2):
                runs = []
                for i in range(4):
                    at = c * 64 + i * 8
                    runs.append(
                        jnp.concatenate(
                            [
                                placed[at : at + 8, h * 128 : h * 128 + 128],
                                placed[at + 32 : at + 40, h * 128 : h * 128 + 128],
                            ],
                            axis=0,
                        )
                    )
                for tt in range(4):
                    t = 4 * h + tt
                    total = None
                    for i in range(4):
                        shift = (32 * (i - tt)) % 128
                        moved = pltpu.roll(runs[i], shift, 1) if shift else runs[i]
                        if total is None:
                            total = moved
                        else:
                            total = jnp.where(lane128 >= 32 * i, moved, total)
                    spec[which, part, c0 + c, t * 8 : t * 8 + 8, 0:128] = total[0:8]
                    spec[which, part, c0 + c, t * 8 : t * 8 + 8, 128:256] = total[8:16]

    loop(0, 16, order)

    loads[3].wait()
    pltpu.make_async_copy(xg, xg, r1).wait()
    high, low = split(xg[...])
    xs[0] = high
    xs[1] = low

    def first_group(q):
        rows = [row_at(row, q, m, 1) for m in range(PER)]
        at = [pl.ds(pl.multiple_of(r * 128, 128), 128) for r in rows]
        wh = jnp.concatenate([first[0, a] for a in at], axis=0)
        wl = jnp.concatenate([first[1, a] for a in at], axis=0)
        value = mm3(wh, wl, xs[0], xs[1])
        for m in range(PER):
            block = value[m * 128 : (m + 1) * 128].reshape(COLS, 2, K1L, B)
            bsend[pl.ds(rows[m] * COLS, COLS)] = block

        @pl.when(q == 0)
        def _():
            pltpu.make_async_copy(bsend.at[me], brecv.at[me], r2.at[q]).start()

        def send(e):
            r = row_at(row, q, lax.rem(e, PER), 1)
            c = col_at(col, lax.div(e, PER))
            pltpu.make_async_remote_copy(
                src_ref=bsend.at[r * COLS + c], dst_ref=brecv.at[me], send_sem=s2,
                recv_sem=r2.at[q], device_id=(r, c), device_id_type=MESH,
            ).start()

        loop(jnp.where(q == 0, 1, 0), PER * COLS, send)

    loop(0, GROUPS, first_group)

    loads[4].wait()

    def inverse(which, q):
        def product(m):
            c = row_at(row, q, m, -1)
            at = pl.ds(pl.multiple_of(m * 64, 64), 64)
            ur, ui = us[q, at, 0:B], us[q, at, B : 2 * B]
            sr, si = spec[which, 0, c], spec[which, 1, c]
            high, low = split(ur * sr + ui * si)
            ah[at, 0:B] = high
            al[at, 0:B] = low
            high, low = split(ui * sr - ur * si)
            ah[at, B : 2 * B] = high
            al[at, B : 2 * B] = low

        loop(0, PER, product)
        vs[...] = mm3(ah[...], al[...], inner[2], inner[3])

        def turn_back(m):
            c = row_at(row, q, m, -1)
            re, im = [], []
            for t in range(RAD):
                at = pl.ds(pl.multiple_of(m * 64 + t * 8, 8), 8)
                r, i = vs[at, 0:B], vs[at, B : 2 * B]
                cs, sn = vt[0, t], vt[1, t]
                re.append(r * cs - i * sn)
                im.append(i * cs + r * sn)
            re, im = dft8(re, im, 1)
            for a in range(RAD):
                r, i = re[a], im[a]
                if a:
                    cs, sn = va[0, a], va[1, a]
                    r, i = r * cs - i * sn, i * cs + r * sn
                tsend[which, c * COLS + a, 0] = r
                tsend[which, c * COLS + a, 1] = i

        loop(0, PER, turn_back)

        @pl.when(q == 0)
        def _():
            pltpu.make_async_copy(tsend.at[which, me], trecv.at[which, me], r4.at[which, q]).start()

        def send(e):
            r = row_at(row, q, lax.rem(e, PER), -1)
            c = col_at(col, lax.div(e, PER))
            pltpu.make_async_remote_copy(
                src_ref=tsend.at[which, r * COLS + c], dst_ref=trecv.at[which, me],
                send_sem=s4.at[which], recv_sem=r4.at[which, q], device_id=(r, c),
                device_id_type=MESH,
            ).start()

        loop(jnp.where(q == 0, 1, 0), PER * COLS, send)

    def forward(q):
        group = brecv.at[pl.ds(0, PER * COLS)]
        pltpu.make_async_copy(group, group, r2.at[q]).wait()

        def outer(m):
            c = row_at(row, q, m, -1)
            re, im = [], []
            for a in range(RAD):
                r, i = brecv[c * COLS + a, 0], brecv[c * COLS + a, 1]
                if a:
                    cs, sn = va[0, a], va[1, a]
                    r, i = r * cs + i * sn, i * cs - r * sn
                re.append(r)
                im.append(i)
            re, im = dft8(re, im, -1)
            out_r, out_i = [], []
            for t in range(RAD):
                cs, sn = vt[0, t], vt[1, t]
                out_r.append(re[t] * cs + im[t] * sn)
                out_i.append(im[t] * cs - re[t] * sn)
            at = pl.ds(pl.multiple_of(m * 64, 64), 64)
            high, low = split(jnp.concatenate(out_r, axis=0))
            ah[at, 0:B] = high
            al[at, 0:B] = low
            high, low = split(jnp.concatenate(out_i, axis=0))
            ah[at, B : 2 * B] = high
            al[at, B : 2 * B] = low

        loop(0, PER, outer)
        us[q] = mm3(ah[...], al[...], inner[0], inner[1])
        inverse(0, q)

    loop(0, GROUPS, forward)
    loop(0, GROUPS, lambda q: inverse(1, q))

    loads[5].wait()

    for which, out in ((0, oh_ref), (1, ox_ref)):

        def last_group(q):
            group = trecv.at[which, pl.ds(0, PER * COLS)]
            pltpu.make_async_copy(group, group, r4.at[which, q]).wait()
            rows = [row_at(row, q, m, 1) for m in range(PER)]
            high, low = split(
                jnp.concatenate(
                    [trecv[which, pl.ds(r * COLS, COLS)].reshape(128, B) for r in rows], axis=0
                )
            )
            wh = jnp.concatenate([last[0, r] for r in rows], axis=1)
            wl = jnp.concatenate([last[1, r] for r in rows], axis=1)
            value = mm3(wh, wl, high, low)

            @pl.when(q == 0)
            def _():
                acc[which] = value

            @pl.when(q > 0)
            def _():
                acc[which] += value

        loop(0, GROUPS, last_group)
        pltpu.make_async_copy(acc.at[which, own_rows], out.at[row], r5.at[which]).start()

        def send_out(i):
            r = lax.rem(row + i, ROWS)
            pltpu.make_async_remote_copy(
                src_ref=acc.at[which, pl.ds(pl.multiple_of(r * N1L, N1L), N1L)],
                dst_ref=out.at[row], send_sem=s5.at[which], recv_sem=r5.at[which],
                device_id=(r, col), device_id_type=MESH,
            ).start()

        loop(1, ROWS, send_out)

    other_rows = xg.at[pl.ds(0, (ROWS - 1) * N1L)]
    pltpu.make_async_copy(other_rows, other_rows, s1).wait()
    others = bsend.at[pl.ds(0, DEVS - 1)]
    pltpu.make_async_copy(others, others, s2).wait()
    for which, out in ((0, oh_ref), (1, ox_ref)):
        others = tsend.at[which, pl.ds(0, DEVS - 1)]
        pltpu.make_async_copy(others, others, s4.at[which]).wait()
        other_rows = acc.at[which, pl.ds(0, (ROWS - 1) * N1L)]
        pltpu.make_async_copy(other_rows, other_rows, s5.at[which]).wait()
        pltpu.make_async_copy(out, out, r5.at[which]).wait()


def local(grad_out, input_spectrum, filter_spectrum):
    first, last, inner, place = (jnp.asarray(t) for t in tables())
    out = jax.ShapeDtypeStruct((CH, N1L, B), F32)
    dma = pltpu.SemaphoreType.DMA
    return pl.pallas_call(
        kernel,
        out_shape=(out, out),
        in_specs=[pl.BlockSpec(memory_space=pl.ANY)] * 7,
        out_specs=(pl.BlockSpec(memory_space=pl.ANY),) * 2,
        scratch_shapes=[
            pltpu.VMEM((2, 2, CH, K1L, N2), F32),
            pltpu.VMEM((2, 2, CH, RAD * K1L, B), F32),
            pltpu.VMEM((2, 2 * N1, HALF1), BF16),
            pltpu.VMEM((2, ROWS, HALF1, 128), BF16),
            pltpu.VMEM((4, 2 * B, 2 * B), BF16),
            pltpu.VMEM((B, B), BF16),
            pltpu.VMEM((HALF1, B), F32),
            pltpu.VMEM((2, HALF1, B), BF16),
            pltpu.VMEM((DEVS, 2, K1L, B), F32),
            pltpu.VMEM((DEVS, 2, K1L, B), F32),
            pltpu.VMEM((2, RAD, K1L, B), F32),
            pltpu.VMEM((2, RAD, K1L, B), F32),
            pltpu.VMEM((PER * 64, 2 * B), BF16),
            pltpu.VMEM((PER * 64, 2 * B), BF16),
            pltpu.VMEM((GROUPS, PER * 64, 2 * B), F32),
            pltpu.VMEM((PER * 64, 2 * B), F32),
            pltpu.VMEM((2, DEVS, 2, K1L, B), F32),
            pltpu.VMEM((2, DEVS, 2, K1L, B), F32),
            pltpu.VMEM((2, HALF1, B), F32),
            dma((6,)),
            dma, dma,
            dma, dma((GROUPS,)),
            dma((2,)), dma((2, GROUPS)),
            dma((2,)), dma((2,)),
        ],
        compiler_params=pltpu.CompilerParams(
            collective_id=0, has_side_effects=True, vmem_limit_bytes=56 * 2**20
        ),
    )(grad_out, input_spectrum, filter_spectrum, first, last, inner, place)


def solution(mesh):
    return jax.shard_map(
        local,
        mesh=mesh,
        in_specs=(
            P(None, "row", "col"),
            P(None, None, ("row", "col"), None),
            P(None, None, ("row", "col"), None),
        ),
        out_specs=(P(None, "row", "col"), P(None, "row", "col")),
        check_vma=False,
    )
```

```python
import functools

import jax
import jax.numpy as jnp
import ml_dtypes
import numpy as np
from jax import lax
from jax.experimental import pallas as pl
from jax.experimental.pallas import tpu as pltpu
from jax.sharding import PartitionSpec as P

MESH = pl.DeviceIdType.MESH
F32 = jnp.float32
BF16 = jnp.bfloat16

ROWS, COLS = 16, 8
DEVS = ROWS * COLS
CH = 16
N1, N2 = 1024, 2048
HALF1 = N1 // 2
TOTAL = N1 * N2
K1L = N1 // DEVS
N1L = HALF1 // ROWS
B = N2 // COLS
RAD = 8
GROUPS, PER = 4, 4
UNITS = ((0, pl.ds(0, B)), (1, pl.ds(0, B // 2)), (1, pl.ds(B // 2, B // 2)))
ROOT_HALF = float(np.sqrt(0.5))


def split_table(table):
    table = np.asarray(table, np.float64)
    high = table.astype(np.float32).astype(ml_dtypes.bfloat16)
    low = (table - high.astype(np.float64)).astype(np.float32).astype(ml_dtypes.bfloat16)
    return np.stack([high, low])


@functools.lru_cache(None)
def tables():
    n1 = np.arange(HALF1)
    k1 = np.arange(N1)
    angle = 2 * np.pi * ((k1[:, None] * n1[None, :]) % N1) / N1
    first = np.stack([np.cos(angle), -np.sin(angle)]).reshape(2, DEVS, K1L, HALF1)
    first = first.transpose(1, 0, 2, 3).reshape(2 * N1, HALF1)
    last = (first.T / TOTAL).reshape(HALF1, ROWS, 2 * N1 // ROWS).transpose(1, 0, 2)
    b = np.arange(B)
    angle = 2 * np.pi * ((b[:, None] * b[None, :]) % B) / B
    c, s = np.cos(angle), np.sin(angle)
    inner = np.block([[c, -s], [s, c]])
    back = np.block([[c, s], [-s, c]])
    place = np.zeros((B, B))
    place[b, (b % RAD) * (B // RAD) + b // RAD] = 1
    return (
        split_table(first),
        split_table(last),
        np.concatenate([split_table(inner), split_table(back)]),
        place.astype(ml_dtypes.bfloat16),
    )


def split(value):
    high = value.astype(BF16)
    low = (value - high.astype(F32)).astype(BF16)
    return high, low


def mm(a, b):
    return jnp.dot(a, b, preferred_element_type=F32)


def mm3(ah, al, bh, bl):
    return mm(ah, bh) + (mm(ah, bl) + mm(al, bh))


def dft4(re, im, sign):
    p0r, p0i = re[0] + re[2], im[0] + im[2]
    p1r, p1i = re[0] - re[2], im[0] - im[2]
    r0r, r0i = re[1] + re[3], im[1] + im[3]
    r1r, r1i = re[1] - re[3], im[1] - im[3]
    out_r = [p0r + r0r, None, p0r - r0r, None]
    out_i = [p0i + r0i, None, p0i - r0i, None]
    if sign > 0:
        out_r[1], out_i[1] = p1r - r1i, p1i + r1r
        out_r[3], out_i[3] = p1r + r1i, p1i - r1r
    else:
        out_r[1], out_i[1] = p1r + r1i, p1i - r1r
        out_r[3], out_i[3] = p1r - r1i, p1i + r1r
    return out_r, out_i


def dft8(re, im, sign):
    ur = [re[a] + re[a + 4] for a in range(4)]
    ui = [im[a] + im[a + 4] for a in range(4)]
    vr = [re[a] - re[a + 4] for a in range(4)]
    vi = [im[a] - im[a + 4] for a in range(4)]
    even_r, even_i = dft4(ur, ui, sign)
    if sign > 0:
        v1 = ((vr[1] - vi[1]) * ROOT_HALF, (vi[1] + vr[1]) * ROOT_HALF)
        v2 = (-vi[2], vr[2])
        v3 = ((vr[3] + vi[3]) * -ROOT_HALF, (vr[3] - vi[3]) * ROOT_HALF)
    else:
        v1 = ((vr[1] + vi[1]) * ROOT_HALF, (vi[1] - vr[1]) * ROOT_HALF)
        v2 = (vi[2], -vr[2])
        v3 = ((vi[3] - vr[3]) * ROOT_HALF, (vr[3] + vi[3]) * -ROOT_HALF)
    odd_r, odd_i = dft4([vr[0], v1[0], v2[0], v3[0]], [vi[0], v1[1], v2[1], v3[1]], sign)
    out_r = [None] * 8
    out_i = [None] * 8
    for t in range(4):
        out_r[2 * t], out_i[2 * t] = even_r[t], even_i[t]
        out_r[2 * t + 1], out_i[2 * t + 1] = odd_r[t], odd_i[t]
    return out_r, out_i


def row_at(row, q, m, way):
    yl, z, core = lax.div(row, 8), lax.rem(lax.div(row, 2), 4), lax.rem(row, 2)
    dyl, dc, dz = lax.div(m, 2), lax.rem(m, 2), lax.rem(q + m, 4)
    dz = dz if way > 0 else 4 - dz
    return lax.rem(yl + dyl, 2) * 8 + lax.rem(z + dz, 4) * 2 + lax.rem(core + dc, 2)


def col_at(col, i):
    yh, x = lax.div(col, 4), lax.rem(col, 4)
    return lax.rem(yh + lax.div(i, 4), 2) * 4 + lax.rem(x + lax.rem(i, 4), 4)


def loop(lower, upper, body):
    def step(i, carry):
        body(i)
        return carry

    lax.fori_loop(lower, upper, step, 0)


def spread(row, col, q, way, send):
    least = jnp.where(q == 0, 1, 0)
    count = PER * COLS - least
    start = (row * COLS + col) * 29

    def step(i):
        e = least + lax.rem(i * 13 + start, count)
        send(row_at(row, q, lax.rem(e, PER), way), col_at(col, lax.div(e, PER)))

    loop(0, count, step)


def kernel(
    grad_ref, sx_ref, sh_ref, first_ref, last_ref, inner_ref, place_ref,
    oh_ref, ox_ref,
    raw, spec, first, last, inner, place, xg, xs, bsend, brecv, va, vt,
    ah, al, us, vs, tsend, trecv, acc,
    lsem, s1, r1, s2, r2, s4, r4, s5, r5,
):
    row = lax.axis_index("row")
    col = lax.axis_index("col")
    me = row * COLS + col

    barrier = pltpu.get_barrier_semaphore()

    def greet(i):
        r = row + i
        r = jnp.where(r >= ROWS, r - ROWS, r)
        for j in range(COLS):
            c = col + j
            c = jnp.where(c >= COLS, c - COLS, c)
            pl.semaphore_signal(barrier, inc=1, device_id=(r, c), device_id_type=MESH)

    for j in range(1, COLS):
        c = col + j
        c = jnp.where(c >= COLS, c - COLS, c)
        pl.semaphore_signal(barrier, inc=1, device_id=(row, c), device_id_type=MESH)
    loop(1, ROWS, greet)

    loads = [
        pltpu.make_async_copy(sh_ref, raw.at[0], lsem.at[0]),
        pltpu.make_async_copy(sx_ref, raw.at[1], lsem.at[1]),
        pltpu.make_async_copy(place_ref, place, lsem.at[2]),
        pltpu.make_async_copy(first_ref, first, lsem.at[3]),
        pltpu.make_async_copy(inner_ref, inner, lsem.at[4]),
        pltpu.make_async_copy(last_ref, last, lsem.at[5]),
    ]
    for load in loads:
        load.start()

    k1 = me * K1L + lax.broadcasted_iota(jnp.int32, (K1L, B), 0)
    lane = lax.broadcasted_iota(jnp.int32, (K1L, B), 1)

    def turn(a):
        phase = lax.rem(k1 * a, TOTAL // B)
        phase = jnp.where(phase > TOTAL // B // 2, phase - TOTAL // B, phase)
        angle = phase.astype(F32) * (2.0 * np.pi * B / TOTAL)
        va[0, a] = jnp.cos(angle)
        va[1, a] = jnp.sin(angle)
        phase = lane * (k1 + N1 * a)
        phase = jnp.where(phase > TOTAL // 2, phase - TOTAL, phase)
        angle = phase.astype(F32) * (2.0 * np.pi / TOTAL)
        vt[0, a] = jnp.cos(angle)
        vt[1, a] = jnp.sin(angle)

    loop(0, RAD, turn)

    pl.semaphore_wait(barrier, DEVS - 1)

    own_rows = pl.ds(pl.multiple_of(row * N1L, N1L), N1L)
    own_x = pltpu.make_async_copy(grad_ref.at[row], xg.at[own_rows], r1)
    own_x.start()

    def send_x(i):
        r = lax.rem(row + i, ROWS)
        pltpu.make_async_remote_copy(
            src_ref=grad_ref.at[r], dst_ref=xg.at[own_rows], send_sem=s1, recv_sem=r1,
            device_id=(r, col), device_id_type=MESH,
        ).start()

    loop(1, ROWS, send_x)

    for load in loads[:3]:
        load.wait()
    lane128 = lax.broadcasted_iota(jnp.int32, (16, 128), 1)

    def order(n):
        which, part, c0 = lax.div(n, 8), lax.rem(lax.div(n, 4), 2), lax.rem(n, 4) * 4
        blocks = []
        for c in range(4):
            whole = raw[which, part, c0 + c]
            blocks += [whole[:, j * B : (j + 1) * B] for j in range(RAD)]
        high, low = split(jnp.concatenate(blocks, axis=0))
        placed = mm(high, place[...]) + mm(low, place[...])
        for c in range(4):
            for h in range(2):
                runs = []
                for i in range(4):
                    at = c * 64 + i * 8
                    runs.append(
                        jnp.concatenate(
                            [
                                placed[at : at + 8, h * 128 : h * 128 + 128],
                                placed[at + 32 : at + 40, h * 128 : h * 128 + 128],
                            ],
                            axis=0,
                        )
                    )
                for tt in range(4):
                    t = 4 * h + tt
                    total = None
                    for i in range(4):
                        shift = (32 * (i - tt)) % 128
                        moved = pltpu.roll(runs[i], shift, 1) if shift else runs[i]
                        if total is None:
                            total = moved
                        else:
                            total = jnp.where(lane128 >= 32 * i, moved, total)
                    spec[which, part, c0 + c, t * 8 : t * 8 + 8, 0:128] = total[0:8]
                    spec[which, part, c0 + c, t * 8 : t * 8 + 8, 128:256] = total[8:16]

    loop(0, 16, order)

    loads[3].wait()
    pltpu.make_async_copy(xg, xg, r1).wait()
    high, low = split(xg[...])
    xs[0] = high
    xs[1] = low

    def first_group(q):
        rows = [row_at(row, q, m, 1) for m in range(PER)]
        at = [pl.ds(pl.multiple_of(r * 128, 128), 128) for r in rows]
        wh = jnp.concatenate([first[0, a] for a in at], axis=0)
        wl = jnp.concatenate([first[1, a] for a in at], axis=0)
        value = mm3(wh, wl, xs[0], xs[1])
        for m in range(PER):
            block = value[m * 128 : (m + 1) * 128].reshape(COLS, 2, K1L, B)
            bsend[pl.ds(rows[m] * COLS, COLS)] = block

        @pl.when(q == 0)
        def _():
            pltpu.make_async_copy(bsend.at[me], brecv.at[me], r2.at[q]).start()

        def send(r, c):
            pltpu.make_async_remote_copy(
                src_ref=bsend.at[r * COLS + c], dst_ref=brecv.at[me], send_sem=s2,
                recv_sem=r2.at[q], device_id=(r, c), device_id_type=MESH,
            ).start()

        spread(row, col, q, 1, send)

    loop(0, GROUPS, first_group)

    loads[4].wait()

    def send_back(unit, q):
        which, lanes = UNITS[unit]

        @pl.when(q == 0)
        def _():
            pltpu.make_async_copy(
                tsend.at[which, me, :, :, lanes], trecv.at[which, me, :, :, lanes], r4.at[unit, q]
            ).start()

        def send(r, c):
            pltpu.make_async_remote_copy(
                src_ref=tsend.at[which, r * COLS + c, :, :, lanes],
                dst_ref=trecv.at[which, me, :, :, lanes],
                send_sem=s4.at[unit], recv_sem=r4.at[unit, q], device_id=(r, c),
                device_id_type=MESH,
            ).start()

        spread(row, col, q, -1, send)

    def inverse(which, q):
        def product(m):
            c = row_at(row, q, m, -1)
            at = pl.ds(pl.multiple_of(m * 64, 64), 64)
            ur, ui = us[q, at, 0:B], us[q, at, B : 2 * B]
            sr, si = spec[which, 0, c], spec[which, 1, c]
            high, low = split(ur * sr + ui * si)
            ah[at, 0:B] = high
            al[at, 0:B] = low
            high, low = split(ui * sr - ur * si)
            ah[at, B : 2 * B] = high
            al[at, B : 2 * B] = low

        loop(0, PER, product)
        vs[...] = mm3(ah[...], al[...], inner[2], inner[3])

        def turn_back(m):
            c = row_at(row, q, m, -1)
            re, im = [], []
            for t in range(RAD):
                at = pl.ds(pl.multiple_of(m * 64 + t * 8, 8), 8)
                r, i = vs[at, 0:B], vs[at, B : 2 * B]
                cs, sn = vt[0, t], vt[1, t]
                re.append(r * cs - i * sn)
                im.append(i * cs + r * sn)
            re, im = dft8(re, im, 1)
            for a in range(RAD):
                r, i = re[a], im[a]
                if a:
                    cs, sn = va[0, a], va[1, a]
                    r, i = r * cs - i * sn, i * cs + r * sn
                tsend[which, c * COLS + a, 0] = r
                tsend[which, c * COLS + a, 1] = i

        loop(0, PER, turn_back)


    def forward(q):
        group = brecv.at[pl.ds(0, PER * COLS)]
        pltpu.make_async_copy(group, group, r2.at[q]).wait()

        def outer(m):
            c = row_at(row, q, m, -1)
            re, im = [], []
            for a in range(RAD):
                r, i = brecv[c * COLS + a, 0], brecv[c * COLS + a, 1]
                if a:
                    cs, sn = va[0, a], va[1, a]
                    r, i = r * cs + i * sn, i * cs - r * sn
                re.append(r)
                im.append(i)
            re, im = dft8(re, im, -1)
            out_r, out_i = [], []
            for t in range(RAD):
                cs, sn = vt[0, t], vt[1, t]
                out_r.append(re[t] * cs + im[t] * sn)
                out_i.append(im[t] * cs - re[t] * sn)
            at = pl.ds(pl.multiple_of(m * 64, 64), 64)
            high, low = split(jnp.concatenate(out_r, axis=0))
            ah[at, 0:B] = high
            al[at, 0:B] = low
            high, low = split(jnp.concatenate(out_i, axis=0))
            ah[at, B : 2 * B] = high
            al[at, B : 2 * B] = low

        loop(0, PER, outer)
        us[q] = mm3(ah[...], al[...], inner[0], inner[1])
        inverse(0, q)
        send_back(0, q)

    def second(q):
        inverse(1, q)
        send_back(1, q)

    loop(0, GROUPS, forward)
    loop(0, GROUPS, second)
    loop(0, GROUPS, lambda q: send_back(2, q))

    loads[5].wait()

    for unit, (which, lanes) in enumerate(UNITS):
        out = (oh_ref, ox_ref)[which]

        def last_group(q):
            group = trecv.at[which, pl.ds(0, PER * COLS), :, :, lanes]
            pltpu.make_async_copy(group, group, r4.at[unit, q]).wait()
            rows = [row_at(row, q, m, 1) for m in range(PER)]
            parts = [trecv[which, pl.ds(r * COLS, COLS), :, :, lanes] for r in rows]
            high, low = split(jnp.concatenate([p.reshape(128, p.shape[-1]) for p in parts], axis=0))
            wh = jnp.concatenate([last[0, r] for r in rows], axis=1)
            wl = jnp.concatenate([last[1, r] for r in rows], axis=1)
            value = mm3(wh, wl, high, low)

            @pl.when(q == 0)
            def _():
                acc[which, :, lanes] = value

            @pl.when(q > 0)
            def _():
                acc[which, :, lanes] += value

        loop(0, GROUPS, last_group)
        pltpu.make_async_copy(
            acc.at[which, own_rows, lanes], out.at[row, :, lanes], r5.at[unit]
        ).start()

        def send_out(i):
            r = lax.rem(row + i, ROWS)
            pltpu.make_async_remote_copy(
                src_ref=acc.at[which, pl.ds(pl.multiple_of(r * N1L, N1L), N1L), lanes],
                dst_ref=out.at[row, :, lanes], send_sem=s5.at[unit], recv_sem=r5.at[unit],
                device_id=(r, col), device_id_type=MESH,
            ).start()

        loop(1, ROWS, send_out)

    other_rows = xg.at[pl.ds(0, (ROWS - 1) * N1L)]
    pltpu.make_async_copy(other_rows, other_rows, s1).wait()
    others = bsend.at[pl.ds(0, DEVS - 1)]
    pltpu.make_async_copy(others, others, s2).wait()
    for unit, (which, lanes) in enumerate(UNITS):
        others = tsend.at[which, pl.ds(0, DEVS - 1), :, :, lanes]
        pltpu.make_async_copy(others, others, s4.at[unit]).wait()
        other_rows = acc.at[which, pl.ds(0, (ROWS - 1) * N1L), lanes]
        pltpu.make_async_copy(other_rows, other_rows, s5.at[unit]).wait()
        out = (oh_ref, ox_ref)[which].at[:, :, lanes]
        pltpu.make_async_copy(out, out, r5.at[unit]).wait()


def hand_over(a_ref, b_ref, c_ref, d_ref, held, in_sem, out_sem):
    pieces = [
        (n, pl.ds(4 * k, 4), source, target)
        for n, (source, target) in enumerate(((a_ref, c_ref), (b_ref, d_ref)))
        for k in range(4)
    ]
    copies = []
    for k, (n, at, source, _) in enumerate(pieces):
        copies.append(pltpu.make_async_copy(source.at[at], held.at[n, at], in_sem.at[k]))
        copies[-1].start()
    back = []
    for k, (n, at, _, target) in enumerate(pieces):
        copies[k].wait()
        back.append(pltpu.make_async_copy(held.at[n, at], target.at[at], out_sem.at[k]))
        back[-1].start()
    for copy in back:
        copy.wait()


def local(grad_out, input_spectrum, filter_spectrum):
    first, last, inner, place = (jnp.asarray(t) for t in tables())
    out = jax.ShapeDtypeStruct((CH, N1L, B), F32)
    dma = pltpu.SemaphoreType.DMA
    results = pl.pallas_call(
        kernel,
        out_shape=(out, out),
        in_specs=[pl.BlockSpec(memory_space=pl.ANY)] * 7,
        out_specs=(pl.BlockSpec(memory_space=pl.ANY),) * 2,
        scratch_shapes=[
            pltpu.VMEM((2, 2, CH, K1L, N2), F32),
            pltpu.VMEM((2, 2, CH, RAD * K1L, B), F32),
            pltpu.VMEM((2, 2 * N1, HALF1), BF16),
            pltpu.VMEM((2, ROWS, HALF1, 128), BF16),
            pltpu.VMEM((4, 2 * B, 2 * B), BF16),
            pltpu.VMEM((B, B), BF16),
            pltpu.VMEM((HALF1, B), F32),
            pltpu.VMEM((2, HALF1, B), BF16),
            pltpu.VMEM((DEVS, 2, K1L, B), F32),
            pltpu.VMEM((DEVS, 2, K1L, B), F32),
            pltpu.VMEM((2, RAD, K1L, B), F32),
            pltpu.VMEM((2, RAD, K1L, B), F32),
            pltpu.VMEM((PER * 64, 2 * B), BF16),
            pltpu.VMEM((PER * 64, 2 * B), BF16),
            pltpu.VMEM((GROUPS, PER * 64, 2 * B), F32),
            pltpu.VMEM((PER * 64, 2 * B), F32),
            pltpu.VMEM((2, DEVS, 2, K1L, B), F32),
            pltpu.VMEM((2, DEVS, 2, K1L, B), F32),
            pltpu.VMEM((2, HALF1, B), F32),
            dma((6,)),
            dma, dma,
            dma, dma((GROUPS,)),
            dma((len(UNITS),)), dma((len(UNITS), GROUPS)),
            dma((len(UNITS),)), dma((len(UNITS),)),
        ],
        compiler_params=pltpu.CompilerParams(
            collective_id=0, has_side_effects=True, vmem_limit_bytes=56 * 2**20
        ),
    )(grad_out, input_spectrum, filter_spectrum, first, last, inner, place)
    return pl.pallas_call(
        hand_over,
        out_shape=(out, out),
        in_specs=[pl.BlockSpec(memory_space=pl.ANY)] * 2,
        out_specs=(pl.BlockSpec(memory_space=pl.ANY),) * 2,
        scratch_shapes=[pltpu.VMEM((2, CH, N1L, B), F32), dma((8,)), dma((8,))],
    )(*results)


def solution(mesh):
    return jax.shard_map(
        local,
        mesh=mesh,
        in_specs=(
            P(None, "row", "col"),
            P(None, None, ("row", "col"), None),
            P(None, None, ("row", "col"), None),
        ),
        out_specs=(P(None, "row", "col"), P(None, "row", "col")),
        check_vma=False,
    )
```

```python
import functools

import jax
import jax.numpy as jnp
import ml_dtypes
import numpy as np
from jax import lax
from jax.experimental import pallas as pl
from jax.experimental.pallas import tpu as pltpu
from jax.sharding import PartitionSpec as P

MESH = pl.DeviceIdType.MESH
F32 = jnp.float32
BF16 = jnp.bfloat16

ROWS, COLS = 16, 8
DEVS = ROWS * COLS
CH = 16
N1, N2 = 1024, 2048
HALF1 = N1 // 2
TOTAL = N1 * N2
K1L = N1 // DEVS
N1L = HALF1 // ROWS
B = N2 // COLS
RAD = 8
GROUPS, PER = 4, 4
UNITS = ((0, pl.ds(0, B)), (1, pl.ds(0, B // 2)), (1, pl.ds(B // 2, B // 2)))
HALVES = (pl.ds(0, B // 2), pl.ds(B // 2, B // 2))
ROOT_HALF = float(np.sqrt(0.5))


def split_table(table):
    table = np.asarray(table, np.float64)
    high = table.astype(np.float32).astype(ml_dtypes.bfloat16)
    low = (table - high.astype(np.float64)).astype(np.float32).astype(ml_dtypes.bfloat16)
    return np.stack([high, low])


@functools.lru_cache(None)
def tables():
    n1 = np.arange(HALF1)
    k1 = np.arange(N1)
    angle = 2 * np.pi * ((k1[:, None] * n1[None, :]) % N1) / N1
    first = np.stack([np.cos(angle), -np.sin(angle)]).reshape(2, DEVS, K1L, HALF1)
    first = first.transpose(1, 0, 2, 3).reshape(2 * N1, HALF1)
    last = (first.T / TOTAL).reshape(HALF1, ROWS, 2 * N1 // ROWS).transpose(1, 0, 2)
    b = np.arange(B)
    angle = 2 * np.pi * ((b[:, None] * b[None, :]) % B) / B
    c, s = np.cos(angle), np.sin(angle)
    inner = np.block([[c, -s], [s, c]])
    back = np.block([[c, s], [-s, c]])
    place = np.zeros((B, B))
    place[b, (b % RAD) * (B // RAD) + b // RAD] = 1
    return (
        split_table(first),
        split_table(last),
        np.concatenate([split_table(inner), split_table(back)]),
        place.astype(ml_dtypes.bfloat16),
    )


def split(value):
    high = value.astype(BF16)
    low = (value - high.astype(F32)).astype(BF16)
    return high, low


def mm(a, b):
    return jnp.dot(a, b, preferred_element_type=F32)


def mm3(ah, al, bh, bl):
    return mm(ah, bh) + (mm(ah, bl) + mm(al, bh))


def dft4(re, im, sign):
    p0r, p0i = re[0] + re[2], im[0] + im[2]
    p1r, p1i = re[0] - re[2], im[0] - im[2]
    r0r, r0i = re[1] + re[3], im[1] + im[3]
    r1r, r1i = re[1] - re[3], im[1] - im[3]
    out_r = [p0r + r0r, None, p0r - r0r, None]
    out_i = [p0i + r0i, None, p0i - r0i, None]
    if sign > 0:
        out_r[1], out_i[1] = p1r - r1i, p1i + r1r
        out_r[3], out_i[3] = p1r + r1i, p1i - r1r
    else:
        out_r[1], out_i[1] = p1r + r1i, p1i - r1r
        out_r[3], out_i[3] = p1r - r1i, p1i + r1r
    return out_r, out_i


def dft8(re, im, sign):
    ur = [re[a] + re[a + 4] for a in range(4)]
    ui = [im[a] + im[a + 4] for a in range(4)]
    vr = [re[a] - re[a + 4] for a in range(4)]
    vi = [im[a] - im[a + 4] for a in range(4)]
    even_r, even_i = dft4(ur, ui, sign)
    if sign > 0:
        v1 = ((vr[1] - vi[1]) * ROOT_HALF, (vi[1] + vr[1]) * ROOT_HALF)
        v2 = (-vi[2], vr[2])
        v3 = ((vr[3] + vi[3]) * -ROOT_HALF, (vr[3] - vi[3]) * ROOT_HALF)
    else:
        v1 = ((vr[1] + vi[1]) * ROOT_HALF, (vi[1] - vr[1]) * ROOT_HALF)
        v2 = (vi[2], -vr[2])
        v3 = ((vi[3] - vr[3]) * ROOT_HALF, (vr[3] + vi[3]) * -ROOT_HALF)
    odd_r, odd_i = dft4([vr[0], v1[0], v2[0], v3[0]], [vi[0], v1[1], v2[1], v3[1]], sign)
    out_r = [None] * 8
    out_i = [None] * 8
    for t in range(4):
        out_r[2 * t], out_i[2 * t] = even_r[t], even_i[t]
        out_r[2 * t + 1], out_i[2 * t + 1] = odd_r[t], odd_i[t]
    return out_r, out_i


def row_at(row, q, m, way):
    yl, z, core = lax.div(row, 8), lax.rem(lax.div(row, 2), 4), lax.rem(row, 2)
    dyl, dc, dz = lax.div(m, 2), lax.rem(m, 2), lax.rem(q + m, 4)
    dz = dz if way > 0 else 4 - dz
    return lax.rem(yl + dyl, 2) * 8 + lax.rem(z + dz, 4) * 2 + lax.rem(core + dc, 2)


def col_at(col, i):
    yh, x = lax.div(col, 4), lax.rem(col, 4)
    return lax.rem(yh + lax.div(i, 4), 2) * 4 + lax.rem(x + lax.rem(i, 4), 4)


def loop(lower, upper, body):
    def step(i, carry):
        body(i)
        return carry

    lax.fori_loop(lower, upper, step, 0)


def spread(row, col, q, way, send):
    least = jnp.where(q == 0, 1, 0)
    count = PER * COLS - least
    start = (row * COLS + col) * 29
    mult = 2 * lax.rem((row * COLS + col) * 7, 15) + 1

    def step(i):
        e = least + lax.rem(i * mult + start, count)
        send(row_at(row, q, lax.rem(e, PER), way), col_at(col, lax.div(e, PER)))

    loop(0, count, step)


def kernel(
    grad_ref, sx_ref, sh_ref, first_ref, last_ref, inner_ref, place_ref,
    oh_ref, ox_ref,
    raw, xin, spec, first, last, inner, place, xg, xs, bsend, brecv, va, vt,
    ah, al, us, vs, tsend, trecv, acc,
    lsem, s1, r1, s2, r2, s4, r4, s5, r5,
):
    row = lax.axis_index("row")
    col = lax.axis_index("col")
    me = row * COLS + col

    barrier = pltpu.get_barrier_semaphore()

    def greet(i):
        r = row + i
        r = jnp.where(r >= ROWS, r - ROWS, r)
        for j in range(COLS):
            c = col + j
            c = jnp.where(c >= COLS, c - COLS, c)
            pl.semaphore_signal(barrier, inc=1, device_id=(r, c), device_id_type=MESH)

    for j in range(1, COLS):
        c = col + j
        c = jnp.where(c >= COLS, c - COLS, c)
        pl.semaphore_signal(barrier, inc=1, device_id=(row, c), device_id_type=MESH)
    loop(1, ROWS, greet)

    load_x = pltpu.make_async_copy(grad_ref, xin, lsem.at[6])
    load_x.start()
    loads = [
        pltpu.make_async_copy(sh_ref, raw.at[0], lsem.at[0]),
        pltpu.make_async_copy(sx_ref, raw.at[1], lsem.at[1]),
        pltpu.make_async_copy(place_ref, place, lsem.at[2]),
        pltpu.make_async_copy(first_ref, first, lsem.at[3]),
        pltpu.make_async_copy(inner_ref, inner, lsem.at[4]),
        pltpu.make_async_copy(last_ref, last, lsem.at[5]),
    ]
    for load in loads:
        load.start()

    k1 = me * K1L + lax.broadcasted_iota(jnp.int32, (K1L, B), 0)
    lane = lax.broadcasted_iota(jnp.int32, (K1L, B), 1)

    def turn(a):
        phase = lax.rem(k1 * a, TOTAL // B)
        phase = jnp.where(phase > TOTAL // B // 2, phase - TOTAL // B, phase)
        angle = phase.astype(F32) * (2.0 * np.pi * B / TOTAL)
        va[0, a] = jnp.cos(angle)
        va[1, a] = jnp.sin(angle)
        phase = lane * (k1 + N1 * a)
        phase = jnp.where(phase > TOTAL // 2, phase - TOTAL, phase)
        angle = phase.astype(F32) * (2.0 * np.pi / TOTAL)
        vt[0, a] = jnp.cos(angle)
        vt[1, a] = jnp.sin(angle)

    loop(0, RAD, turn)

    pl.semaphore_wait(barrier, DEVS - 1)

    own_rows = pl.ds(pl.multiple_of(row * N1L, N1L), N1L)
    load_x.wait()
    for h, lanes in enumerate(HALVES):
        pltpu.make_async_copy(xin.at[row, :, lanes], xg.at[own_rows, lanes], r1.at[h]).start()

        def send_x(i):
            r = row + i
            r = jnp.where(r >= ROWS, r - ROWS, r)
            pltpu.make_async_remote_copy(
                src_ref=xin.at[r, :, lanes], dst_ref=xg.at[own_rows, lanes], send_sem=s1,
                recv_sem=r1.at[h], device_id=(r, col), device_id_type=MESH,
            ).start()

        loop(1, ROWS, send_x)

    for load in loads[:3]:
        load.wait()
    lane128 = lax.broadcasted_iota(jnp.int32, (16, 128), 1)

    def order(n):
        which, part, c0 = lax.div(n, 8), lax.rem(lax.div(n, 4), 2), lax.rem(n, 4) * 4
        blocks = []
        for c in range(4):
            whole = raw[which, part, c0 + c]
            blocks += [whole[:, j * B : (j + 1) * B] for j in range(RAD)]
        high, low = split(jnp.concatenate(blocks, axis=0))
        placed = mm(high, place[...]) + mm(low, place[...])
        for c in range(4):
            for h in range(2):
                runs = []
                for i in range(4):
                    at = c * 64 + i * 8
                    runs.append(
                        jnp.concatenate(
                            [
                                placed[at : at + 8, h * 128 : h * 128 + 128],
                                placed[at + 32 : at + 40, h * 128 : h * 128 + 128],
                            ],
                            axis=0,
                        )
                    )
                for tt in range(4):
                    t = 4 * h + tt
                    total = None
                    for i in range(4):
                        shift = (32 * (i - tt)) % 128
                        moved = pltpu.roll(runs[i], shift, 1) if shift else runs[i]
                        if total is None:
                            total = moved
                        else:
                            total = jnp.where(lane128 >= 32 * i, moved, total)
                    spec[which, part, c0 + c, t * 8 : t * 8 + 8, 0:128] = total[0:8]
                    spec[which, part, c0 + c, t * 8 : t * 8 + 8, 128:256] = total[8:16]

    loop(0, 16, order)

    loads[3].wait()
    for h, lanes in enumerate(HALVES):
        arrived = xg.at[:, lanes]
        pltpu.make_async_copy(arrived, arrived, r1.at[h]).wait()
        high, low = split(xg[:, lanes])
        xs[0, h] = high
        xs[1, h] = low

        def first_group(q):
            rows = [row_at(row, q, m, 1) for m in range(PER)]
            at = [pl.ds(pl.multiple_of(r * 128, 128), 128) for r in rows]
            wh = jnp.concatenate([first[0, a] for a in at], axis=0)
            wl = jnp.concatenate([first[1, a] for a in at], axis=0)
            value = mm3(wh, wl, xs[0, h], xs[1, h])
            for m in range(PER):
                block = value[m * 128 : (m + 1) * 128].reshape(COLS, 2, K1L, B // 2)
                bsend[pl.ds(rows[m] * COLS, COLS), :, :, lanes] = block

            @pl.when(q == 0)
            def _():
                pltpu.make_async_copy(
                    bsend.at[me, :, :, lanes], brecv.at[me, :, :, lanes], r2.at[q]
                ).start()

            def send(r, c):
                pltpu.make_async_remote_copy(
                    src_ref=bsend.at[r * COLS + c, :, :, lanes], dst_ref=brecv.at[me, :, :, lanes],
                    send_sem=s2, recv_sem=r2.at[q], device_id=(r, c), device_id_type=MESH,
                ).start()

            spread(row, col, q, 1, send)

        loop(0, GROUPS, first_group)

    loads[4].wait()

    def send_back(unit, q):
        which, lanes = UNITS[unit]

        @pl.when(q == 0)
        def _():
            pltpu.make_async_copy(
                tsend.at[which, me, :, :, lanes], trecv.at[which, me, :, :, lanes], r4.at[unit, q]
            ).start()

        def send(r, c):
            pltpu.make_async_remote_copy(
                src_ref=tsend.at[which, r * COLS + c, :, :, lanes],
                dst_ref=trecv.at[which, me, :, :, lanes],
                send_sem=s4.at[unit], recv_sem=r4.at[unit, q], device_id=(r, c),
                device_id_type=MESH,
            ).start()

        spread(row, col, q, -1, send)

    def inverse(which, q):
        def product(m):
            c = row_at(row, q, m, -1)
            at = pl.ds(pl.multiple_of(m * 64, 64), 64)
            ur, ui = us[q, at, 0:B], us[q, at, B : 2 * B]
            sr, si = spec[which, 0, c], spec[which, 1, c]
            high, low = split(ur * sr + ui * si)
            ah[at, 0:B] = high
            al[at, 0:B] = low
            high, low = split(ui * sr - ur * si)
            ah[at, B : 2 * B] = high
            al[at, B : 2 * B] = low

        loop(0, PER, product)
        vs[...] = mm3(ah[...], al[...], inner[2], inner[3])

        def turn_back(m):
            c = row_at(row, q, m, -1)
            re, im = [], []
            for t in range(RAD):
                at = pl.ds(pl.multiple_of(m * 64 + t * 8, 8), 8)
                r, i = vs[at, 0:B], vs[at, B : 2 * B]
                cs, sn = vt[0, t], vt[1, t]
                re.append(r * cs - i * sn)
                im.append(i * cs + r * sn)
            re, im = dft8(re, im, 1)
            for a in range(RAD):
                r, i = re[a], im[a]
                if a:
                    cs, sn = va[0, a], va[1, a]
                    r, i = r * cs - i * sn, i * cs + r * sn
                tsend[which, c * COLS + a, 0] = r
                tsend[which, c * COLS + a, 1] = i

        loop(0, PER, turn_back)


    def forward(q):
        group = brecv.at[pl.ds(0, PER * COLS)]
        pltpu.make_async_copy(group, group, r2.at[q]).wait()

        def outer(m):
            c = row_at(row, q, m, -1)
            re, im = [], []
            for a in range(RAD):
                r, i = brecv[c * COLS + a, 0], brecv[c * COLS + a, 1]
                if a:
                    cs, sn = va[0, a], va[1, a]
                    r, i = r * cs + i * sn, i * cs - r * sn
                re.append(r)
                im.append(i)
            re, im = dft8(re, im, -1)
            out_r, out_i = [], []
            for t in range(RAD):
                cs, sn = vt[0, t], vt[1, t]
                out_r.append(re[t] * cs + im[t] * sn)
                out_i.append(im[t] * cs - re[t] * sn)
            at = pl.ds(pl.multiple_of(m * 64, 64), 64)
            high, low = split(jnp.concatenate(out_r, axis=0))
            ah[at, 0:B] = high
            al[at, 0:B] = low
            high, low = split(jnp.concatenate(out_i, axis=0))
            ah[at, B : 2 * B] = high
            al[at, B : 2 * B] = low

        loop(0, PER, outer)
        us[q] = mm3(ah[...], al[...], inner[0], inner[1])
        inverse(0, q)
        send_back(0, q)

    def second(q):
        inverse(1, q)
        send_back(1, q)

    loop(0, GROUPS, forward)
    loop(0, GROUPS, second)
    loop(0, GROUPS, lambda q: send_back(2, q))

    loads[5].wait()

    for unit, (which, lanes) in enumerate(UNITS):
        out = (oh_ref, ox_ref)[which]

        def gathered(q):
            group = trecv.at[which, pl.ds(0, PER * COLS), :, :, lanes]
            pltpu.make_async_copy(group, group, r4.at[unit, q]).wait()
            rows = [row_at(row, q, m, 1) for m in range(PER)]
            parts = [trecv[which, pl.ds(r * COLS, COLS), :, :, lanes] for r in rows]
            whole = jnp.concatenate([p.reshape(128, p.shape[-1]) for p in parts], axis=0)
            return rows, *split(whole)

        def added(rows, at, high, low):
            wh = jnp.concatenate([last[0, r, at] for r in rows], axis=1)
            wl = jnp.concatenate([last[1, r, at] for r in rows], axis=1)
            return mm3(wh, wl, high, low)

        def last_group(q):
            rows, high, low = gathered(q)
            value = added(rows, pl.ds(0, HALF1), high, low)

            @pl.when(q == 0)
            def _():
                acc[which, :, lanes] = value

            @pl.when(q > 0)
            def _():
                acc[which, :, lanes] += value

        loop(0, GROUPS - 1, last_group)

        rows, high, low = gathered(GROUPS - 1)

        def finish(k):
            half = lax.rem(lax.div(row, ROWS // 2) + k, 2)
            at = pl.ds(pl.multiple_of(half * (HALF1 // 2), HALF1 // 2), HALF1 // 2)
            acc[which, at, lanes] += added(rows, at, high, low)

            @pl.when(k == 0)
            def _():
                pltpu.make_async_copy(
                    acc.at[which, own_rows, lanes], out.at[row, :, lanes], r5.at[unit]
                ).start()

            def send_out(i):
                r = half * (ROWS // 2) + lax.rem(row + i, ROWS // 2)
                pltpu.make_async_remote_copy(
                    src_ref=acc.at[which, pl.ds(pl.multiple_of(r * N1L, N1L), N1L), lanes],
                    dst_ref=out.at[row, :, lanes], send_sem=s5.at[unit], recv_sem=r5.at[unit],
                    device_id=(r, col), device_id_type=MESH,
                ).start()

            loop(jnp.where(k == 0, 1, 0), ROWS // 2, send_out)

        loop(0, 2, finish)

    other_rows = xg.at[pl.ds(0, (ROWS - 1) * N1L)]
    pltpu.make_async_copy(other_rows, other_rows, s1).wait()
    others = bsend.at[pl.ds(0, DEVS - 1)]
    pltpu.make_async_copy(others, others, s2).wait()
    for unit, (which, lanes) in enumerate(UNITS):
        others = tsend.at[which, pl.ds(0, DEVS - 1), :, :, lanes]
        pltpu.make_async_copy(others, others, s4.at[unit]).wait()
        other_rows = acc.at[which, pl.ds(0, (ROWS - 1) * N1L), lanes]
        pltpu.make_async_copy(other_rows, other_rows, s5.at[unit]).wait()
        out = (oh_ref, ox_ref)[which].at[:, :, lanes]
        pltpu.make_async_copy(out, out, r5.at[unit]).wait()


def hand_over(a_ref, b_ref, c_ref, d_ref, held, in_sem, out_sem):
    pieces = [
        (n, pl.ds(4 * k, 4), source, target)
        for n, (source, target) in enumerate(((a_ref, c_ref), (b_ref, d_ref)))
        for k in range(4)
    ]
    copies = []
    for k, (n, at, source, _) in enumerate(pieces):
        copies.append(pltpu.make_async_copy(source.at[at], held.at[n, at], in_sem.at[k]))
        copies[-1].start()
    back = []
    for k, (n, at, _, target) in enumerate(pieces):
        copies[k].wait()
        back.append(pltpu.make_async_copy(held.at[n, at], target.at[at], out_sem.at[k]))
        back[-1].start()
    for copy in back:
        copy.wait()


def local(grad_out, input_spectrum, filter_spectrum):
    first, last, inner, place = (jnp.asarray(t) for t in tables())
    out = jax.ShapeDtypeStruct((CH, N1L, B), F32)
    dma = pltpu.SemaphoreType.DMA
    results = pl.pallas_call(
        kernel,
        out_shape=(out, out),
        in_specs=[pl.BlockSpec(memory_space=pl.ANY)] * 7,
        out_specs=(pl.BlockSpec(memory_space=pl.ANY),) * 2,
        scratch_shapes=[
            pltpu.VMEM((2, 2, CH, K1L, N2), F32),
            pltpu.VMEM((CH, N1L, B), F32),
            pltpu.VMEM((2, 2, CH, RAD * K1L, B), F32),
            pltpu.VMEM((2, 2 * N1, HALF1), BF16),
            pltpu.VMEM((2, ROWS, HALF1, 128), BF16),
            pltpu.VMEM((4, 2 * B, 2 * B), BF16),
            pltpu.VMEM((B, B), BF16),
            pltpu.VMEM((HALF1, B), F32),
            pltpu.VMEM((2, 2, HALF1, B // 2), BF16),
            pltpu.VMEM((DEVS, 2, K1L, B), F32),
            pltpu.VMEM((DEVS, 2, K1L, B), F32),
            pltpu.VMEM((2, RAD, K1L, B), F32),
            pltpu.VMEM((2, RAD, K1L, B), F32),
            pltpu.VMEM((PER * 64, 2 * B), BF16),
            pltpu.VMEM((PER * 64, 2 * B), BF16),
            pltpu.VMEM((GROUPS, PER * 64, 2 * B), F32),
            pltpu.VMEM((PER * 64, 2 * B), F32),
            pltpu.VMEM((2, DEVS, 2, K1L, B), F32),
            pltpu.VMEM((2, DEVS, 2, K1L, B), F32),
            pltpu.VMEM((2, HALF1, B), F32),
            dma((7,)),
            dma, dma((2,)),
            dma, dma((GROUPS,)),
            dma((len(UNITS),)), dma((len(UNITS), GROUPS)),
            dma((len(UNITS),)), dma((len(UNITS),)),
        ],
        compiler_params=pltpu.CompilerParams(
            collective_id=0, has_side_effects=True, vmem_limit_bytes=56 * 2**20
        ),
    )(grad_out, input_spectrum, filter_spectrum, first, last, inner, place)
    return pl.pallas_call(
        hand_over,
        out_shape=(out, out),
        in_specs=[pl.BlockSpec(memory_space=pl.ANY)] * 2,
        out_specs=(pl.BlockSpec(memory_space=pl.ANY),) * 2,
        scratch_shapes=[pltpu.VMEM((2, CH, N1L, B), F32), dma((8,)), dma((8,))],
    )(*results)


def solution(mesh):
    return jax.shard_map(
        local,
        mesh=mesh,
        in_specs=(
            P(None, "row", "col"),
            P(None, None, ("row", "col"), None),
            P(None, None, ("row", "col"), None),
        ),
        out_specs=(P(None, "row", "col"), P(None, "row", "col")),
        check_vma=False,
    )
```

```python
import functools

import jax
import jax.numpy as jnp
import ml_dtypes
import numpy as np
from jax import lax
from jax.experimental import pallas as pl
from jax.experimental.pallas import tpu as pltpu
from jax.sharding import PartitionSpec as P

MESH = pl.DeviceIdType.MESH
F32 = jnp.float32
BF16 = jnp.bfloat16

ROWS, COLS = 16, 8
DEVS = ROWS * COLS
CH = 16
N1, N2 = 1024, 2048
HALF1 = N1 // 2
TOTAL = N1 * N2
K1L = N1 // DEVS
N1L = HALF1 // ROWS
B = N2 // COLS
RAD = 8
GROUPS, PER = 4, 4
UNITS = ((0, pl.ds(0, B)), (1, pl.ds(0, B)))
HALVES = (pl.ds(0, B // 2), pl.ds(B // 2, B // 2))
ROOT_HALF = float(np.sqrt(0.5))


def split_table(table):
    table = np.asarray(table, np.float64)
    high = table.astype(np.float32).astype(ml_dtypes.bfloat16)
    low = (table - high.astype(np.float64)).astype(np.float32).astype(ml_dtypes.bfloat16)
    return np.stack([high, low])


@functools.lru_cache(None)
def tables():
    n1 = np.arange(HALF1)
    k1 = np.arange(N1)
    angle = 2 * np.pi * ((k1[:, None] * n1[None, :]) % N1) / N1
    first = np.stack([np.cos(angle), -np.sin(angle)]).reshape(2, DEVS, K1L, HALF1)
    first = first.transpose(1, 0, 2, 3).reshape(2 * N1, HALF1)
    last = (first.T / TOTAL).reshape(HALF1, ROWS, 2 * N1 // ROWS).transpose(1, 0, 2)
    b = np.arange(B)
    angle = 2 * np.pi * ((b[:, None] * b[None, :]) % B) / B
    c, s = np.cos(angle), np.sin(angle)
    inner = np.block([[c, -s], [s, c]])
    back = np.block([[c, s], [-s, c]])
    place = np.zeros((B, B))
    place[b, (b % RAD) * (B // RAD) + b // RAD] = 1
    return (
        split_table(first),
        split_table(last),
        np.concatenate([split_table(inner), split_table(back)]),
        place.astype(ml_dtypes.bfloat16),
    )


def split(value):
    high = value.astype(BF16)
    low = (value - high.astype(F32)).astype(BF16)
    return high, low


def mm(a, b):
    return jnp.dot(a, b, preferred_element_type=F32)


def mm3(ah, al, bh, bl):
    return mm(ah, bh) + (mm(ah, bl) + mm(al, bh))


def dft4(re, im, sign):
    p0r, p0i = re[0] + re[2], im[0] + im[2]
    p1r, p1i = re[0] - re[2], im[0] - im[2]
    r0r, r0i = re[1] + re[3], im[1] + im[3]
    r1r, r1i = re[1] - re[3], im[1] - im[3]
    out_r = [p0r + r0r, None, p0r - r0r, None]
    out_i = [p0i + r0i, None, p0i - r0i, None]
    if sign > 0:
        out_r[1], out_i[1] = p1r - r1i, p1i + r1r
        out_r[3], out_i[3] = p1r + r1i, p1i - r1r
    else:
        out_r[1], out_i[1] = p1r + r1i, p1i - r1r
        out_r[3], out_i[3] = p1r - r1i, p1i + r1r
    return out_r, out_i


def dft8(re, im, sign):
    ur = [re[a] + re[a + 4] for a in range(4)]
    ui = [im[a] + im[a + 4] for a in range(4)]
    vr = [re[a] - re[a + 4] for a in range(4)]
    vi = [im[a] - im[a + 4] for a in range(4)]
    even_r, even_i = dft4(ur, ui, sign)
    if sign > 0:
        v1 = ((vr[1] - vi[1]) * ROOT_HALF, (vi[1] + vr[1]) * ROOT_HALF)
        v2 = (-vi[2], vr[2])
        v3 = ((vr[3] + vi[3]) * -ROOT_HALF, (vr[3] - vi[3]) * ROOT_HALF)
    else:
        v1 = ((vr[1] + vi[1]) * ROOT_HALF, (vi[1] - vr[1]) * ROOT_HALF)
        v2 = (vi[2], -vr[2])
        v3 = ((vi[3] - vr[3]) * ROOT_HALF, (vr[3] + vi[3]) * -ROOT_HALF)
    odd_r, odd_i = dft4([vr[0], v1[0], v2[0], v3[0]], [vi[0], v1[1], v2[1], v3[1]], sign)
    out_r = [None] * 8
    out_i = [None] * 8
    for t in range(4):
        out_r[2 * t], out_i[2 * t] = even_r[t], even_i[t]
        out_r[2 * t + 1], out_i[2 * t + 1] = odd_r[t], odd_i[t]
    return out_r, out_i


def row_at(row, q, m, way):
    yl, z, core = lax.div(row, 8), lax.rem(lax.div(row, 2), 4), lax.rem(row, 2)
    dyl, dc, dz = lax.div(m, 2), lax.rem(m, 2), lax.rem(q + m, 4)
    dz = dz if way > 0 else 4 - dz
    return lax.rem(yl + dyl, 2) * 8 + lax.rem(z + dz, 4) * 2 + lax.rem(core + dc, 2)


def col_at(col, i):
    yh, x = lax.div(col, 4), lax.rem(col, 4)
    return lax.rem(yh + lax.div(i, 4), 2) * 4 + lax.rem(x + lax.rem(i, 4), 4)


def loop(lower, upper, body):
    def step(i, carry):
        body(i)
        return carry

    lax.fori_loop(lower, upper, step, 0)


def spread(row, col, q, way, send):
    turn = row + col + lax.div(row, 4)
    rows = [row_at(row, q, lax.rem(m + turn, PER), way) for m in range(PER)]
    step = 2 * lax.rem(row, 4) + 1
    start = row * 3 + col * 5 + lax.div(row, 4)

    def visit(i):
        base = i * step + start
        for m, r in enumerate(rows):
            c = lax.rem(base + 3 * m, COLS)
            pl.when((r != row) | (c != col))(functools.partial(send, r, c))

    loop(0, COLS, visit)


def kernel(
    grad_ref, sx_ref, sh_ref, first_ref, last_ref, inner_ref, place_ref,
    oh_ref, ox_ref,
    raw, xin, spec, first, last, inner, place, xg, xs, bsend, brecv, va, vt,
    ah, al, us, vs, tsend, trecv, acc,
    lsem, s1, r1, s2, r2, s4, r4, s5, r5,
):
    row = lax.axis_index("row")
    col = lax.axis_index("col")
    me = row * COLS + col

    barrier = pltpu.get_barrier_semaphore()

    def greet(i):
        r = row + i
        r = jnp.where(r >= ROWS, r - ROWS, r)
        for j in range(COLS):
            c = col + j
            c = jnp.where(c >= COLS, c - COLS, c)
            pl.semaphore_signal(barrier, inc=1, device_id=(r, c), device_id_type=MESH)

    for j in range(1, COLS):
        c = col + j
        c = jnp.where(c >= COLS, c - COLS, c)
        pl.semaphore_signal(barrier, inc=1, device_id=(row, c), device_id_type=MESH)
    loop(1, ROWS, greet)

    load_x = pltpu.make_async_copy(grad_ref, xin, lsem.at[6])
    load_x.start()
    loads = [
        pltpu.make_async_copy(sh_ref, raw.at[0], lsem.at[0]),
        pltpu.make_async_copy(sx_ref, raw.at[1], lsem.at[1]),
        pltpu.make_async_copy(place_ref, place, lsem.at[2]),
        pltpu.make_async_copy(first_ref, first, lsem.at[3]),
        pltpu.make_async_copy(inner_ref, inner, lsem.at[4]),
        pltpu.make_async_copy(last_ref, last, lsem.at[5]),
    ]
    for load in loads:
        load.start()

    k1 = me * K1L + lax.broadcasted_iota(jnp.int32, (K1L, B), 0)
    lane = lax.broadcasted_iota(jnp.int32, (K1L, B), 1)

    def turn(a):
        phase = lax.rem(k1 * a, TOTAL // B)
        phase = jnp.where(phase > TOTAL // B // 2, phase - TOTAL // B, phase)
        angle = phase.astype(F32) * (2.0 * np.pi * B / TOTAL)
        va[0, a] = jnp.cos(angle)
        va[1, a] = jnp.sin(angle)
        phase = lane * (k1 + N1 * a)
        phase = jnp.where(phase > TOTAL // 2, phase - TOTAL, phase)
        angle = phase.astype(F32) * (2.0 * np.pi / TOTAL)
        vt[0, a] = jnp.cos(angle)
        vt[1, a] = jnp.sin(angle)

    loop(0, RAD, turn)

    pl.semaphore_wait(barrier, DEVS - 1)

    own_rows = pl.ds(pl.multiple_of(row * N1L, N1L), N1L)
    load_x.wait()
    for h, lanes in enumerate(HALVES):
        pltpu.make_async_copy(xin.at[row, :, lanes], xg.at[own_rows, lanes], r1.at[h]).start()

        def send_x(n):
            r = 2 * lax.rem(lax.div(row, 2) + lax.rem(n, ROWS // 2), ROWS // 2) + lax.div(n, ROWS // 2)

            @pl.when(r != row)
            def _():
                pltpu.make_async_remote_copy(
                    src_ref=xin.at[r, :, lanes], dst_ref=xg.at[own_rows, lanes], send_sem=s1,
                    recv_sem=r1.at[h], device_id=(r, col), device_id_type=MESH,
                ).start()

        loop(0, ROWS, send_x)

    lane128 = lax.broadcasted_iota(jnp.int32, (16, 128), 1)

    def order(n):
        which, part, c0 = lax.div(n, 8), lax.rem(lax.div(n, 4), 2), lax.rem(n, 4) * 4
        blocks = []
        for c in range(4):
            whole = raw[which, part, c0 + c]
            blocks += [whole[:, j * B : (j + 1) * B] for j in range(RAD)]
        high, low = split(jnp.concatenate(blocks, axis=0))
        placed = mm(high, place[...]) + mm(low, place[...])
        for c in range(4):
            for h in range(2):
                runs = []
                for i in range(4):
                    at = c * 64 + i * 8
                    runs.append(
                        jnp.concatenate(
                            [
                                placed[at : at + 8, h * 128 : h * 128 + 128],
                                placed[at + 32 : at + 40, h * 128 : h * 128 + 128],
                            ],
                            axis=0,
                        )
                    )
                for tt in range(4):
                    t = 4 * h + tt
                    total = None
                    for i in range(4):
                        shift = (32 * (i - tt)) % 128
                        moved = pltpu.roll(runs[i], shift, 1) if shift else runs[i]
                        if total is None:
                            total = moved
                        else:
                            total = jnp.where(lane128 >= 32 * i, moved, total)
                    spec[which, part, c0 + c, t * 8 : t * 8 + 8, 0:128] = total[0:8]
                    spec[which, part, c0 + c, t * 8 : t * 8 + 8, 128:256] = total[8:16]


    loads[3].wait()
    for h, lanes in enumerate(HALVES):
        arrived = xg.at[:, lanes]
        pltpu.make_async_copy(arrived, arrived, r1.at[h]).wait()
        high, low = split(xg[:, lanes])
        xs[0, h] = high
        xs[1, h] = low

        def first_group(q):
            rows = [row_at(row, q, m, 1) for m in range(PER)]
            at = [pl.ds(pl.multiple_of(r * 128, 128), 128) for r in rows]
            wh = jnp.concatenate([first[0, a] for a in at], axis=0)
            wl = jnp.concatenate([first[1, a] for a in at], axis=0)
            value = mm3(wh, wl, xs[0, h], xs[1, h])
            for m in range(PER):
                block = value[m * 128 : (m + 1) * 128].reshape(COLS, 2, K1L, B // 2)
                bsend[pl.ds(rows[m] * COLS, COLS), :, :, lanes] = block

            @pl.when(q == 0)
            def _():
                pltpu.make_async_copy(
                    bsend.at[me, :, :, lanes], brecv.at[me, :, :, lanes], r2.at[q]
                ).start()

            def send(r, c):
                pltpu.make_async_remote_copy(
                    src_ref=bsend.at[r * COLS + c, :, :, lanes], dst_ref=brecv.at[me, :, :, lanes],
                    send_sem=s2, recv_sem=r2.at[q], device_id=(r, c), device_id_type=MESH,
                ).start()

            spread(row, col, q, 1, send)

        loop(0, GROUPS, first_group)

    for load in loads[:3]:
        load.wait()
    loop(0, 16, order)
    loads[4].wait()

    def send_back(unit, q):
        which, lanes = UNITS[unit]

        @pl.when(q == 0)
        def _():
            pltpu.make_async_copy(
                tsend.at[which, me, :, :, lanes], trecv.at[which, me, :, :, lanes], r4.at[unit, q]
            ).start()

        def send(r, c):
            pltpu.make_async_remote_copy(
                src_ref=tsend.at[which, r * COLS + c, :, :, lanes],
                dst_ref=trecv.at[which, me, :, :, lanes],
                send_sem=s4.at[unit], recv_sem=r4.at[unit, q], device_id=(r, c),
                device_id_type=MESH,
            ).start()

        spread(row, col, q, -1, send)

    def inverse(which, q):
        def product(m):
            c = row_at(row, q, m, -1)
            at = pl.ds(pl.multiple_of(m * 64, 64), 64)
            ur, ui = us[q, at, 0:B], us[q, at, B : 2 * B]
            sr, si = spec[which, 0, c], spec[which, 1, c]
            high, low = split(ur * sr + ui * si)
            ah[at, 0:B] = high
            al[at, 0:B] = low
            high, low = split(ui * sr - ur * si)
            ah[at, B : 2 * B] = high
            al[at, B : 2 * B] = low

        loop(0, PER, product)
        vs[...] = mm3(ah[...], al[...], inner[2], inner[3])

        def turn_back(m):
            c = row_at(row, q, m, -1)
            re, im = [], []
            for t in range(RAD):
                at = pl.ds(pl.multiple_of(m * 64 + t * 8, 8), 8)
                r, i = vs[at, 0:B], vs[at, B : 2 * B]
                cs, sn = vt[0, t], vt[1, t]
                re.append(r * cs - i * sn)
                im.append(i * cs + r * sn)
            re, im = dft8(re, im, 1)
            for a in range(RAD):
                r, i = re[a], im[a]
                if a:
                    cs, sn = va[0, a], va[1, a]
                    r, i = r * cs - i * sn, i * cs + r * sn
                tsend[which, c * COLS + a, 0] = r
                tsend[which, c * COLS + a, 1] = i

        loop(0, PER, turn_back)


    def forward(q):
        group = brecv.at[pl.ds(0, PER * COLS)]
        pltpu.make_async_copy(group, group, r2.at[q]).wait()

        def outer(m):
            c = row_at(row, q, m, -1)
            re, im = [], []
            for a in range(RAD):
                r, i = brecv[c * COLS + a, 0], brecv[c * COLS + a, 1]
                if a:
                    cs, sn = va[0, a], va[1, a]
                    r, i = r * cs + i * sn, i * cs - r * sn
                re.append(r)
                im.append(i)
            re, im = dft8(re, im, -1)
            out_r, out_i = [], []
            for t in range(RAD):
                cs, sn = vt[0, t], vt[1, t]
                out_r.append(re[t] * cs + im[t] * sn)
                out_i.append(im[t] * cs - re[t] * sn)
            at = pl.ds(pl.multiple_of(m * 64, 64), 64)
            high, low = split(jnp.concatenate(out_r, axis=0))
            ah[at, 0:B] = high
            al[at, 0:B] = low
            high, low = split(jnp.concatenate(out_i, axis=0))
            ah[at, B : 2 * B] = high
            al[at, B : 2 * B] = low

        loop(0, PER, outer)
        us[q] = mm3(ah[...], al[...], inner[0], inner[1])
        inverse(0, q)
        send_back(0, q)

    def second(q):
        inverse(1, q)
        send_back(1, q)

    loop(0, GROUPS, forward)
    loop(0, GROUPS, second)

    loads[5].wait()

    for unit, (which, lanes) in enumerate(UNITS):
        out = (oh_ref, ox_ref)[which]

        def gathered(q):
            group = trecv.at[which, pl.ds(0, PER * COLS), :, :, lanes]
            pltpu.make_async_copy(group, group, r4.at[unit, q]).wait()
            rows = [row_at(row, q, m, 1) for m in range(PER)]
            parts = [trecv[which, pl.ds(r * COLS, COLS), :, :, lanes] for r in rows]
            whole = jnp.concatenate([p.reshape(128, p.shape[-1]) for p in parts], axis=0)
            return rows, *split(whole)

        def added(rows, at, high, low):
            wh = jnp.concatenate([last[0, r, at] for r in rows], axis=1)
            wl = jnp.concatenate([last[1, r, at] for r in rows], axis=1)
            return mm3(wh, wl, high, low)

        def last_group(q):
            rows, high, low = gathered(q)
            value = added(rows, pl.ds(0, HALF1), high, low)

            @pl.when(q == 0)
            def _():
                acc[which, :, lanes] = value

            @pl.when(q > 0)
            def _():
                acc[which, :, lanes] += value

        loop(0, GROUPS - 1, last_group)

        rows, high, low = gathered(GROUPS - 1)

        def finish(k):
            half = lax.rem(lax.div(row, ROWS // 2) + k, 2)
            at = pl.ds(pl.multiple_of(half * (HALF1 // 2), HALF1 // 2), HALF1 // 2)
            acc[which, at, lanes] += added(rows, at, high, low)

            @pl.when(k == 0)
            def _():
                pltpu.make_async_copy(
                    acc.at[which, own_rows, lanes], out.at[row, :, lanes], r5.at[unit]
                ).start()

            def send_out(i):
                r = half * (ROWS // 2) + lax.rem(row + i, ROWS // 2)
                pltpu.make_async_remote_copy(
                    src_ref=acc.at[which, pl.ds(pl.multiple_of(r * N1L, N1L), N1L), lanes],
                    dst_ref=out.at[row, :, lanes], send_sem=s5.at[unit], recv_sem=r5.at[unit],
                    device_id=(r, col), device_id_type=MESH,
                ).start()

            loop(jnp.where(k == 0, 1, 0), ROWS // 2, send_out)

        loop(0, 2, finish)

    other_rows = xg.at[pl.ds(0, (ROWS - 1) * N1L)]
    pltpu.make_async_copy(other_rows, other_rows, s1).wait()
    others = bsend.at[pl.ds(0, DEVS - 1)]
    pltpu.make_async_copy(others, others, s2).wait()
    for unit, (which, lanes) in enumerate(UNITS):
        others = tsend.at[which, pl.ds(0, DEVS - 1), :, :, lanes]
        pltpu.make_async_copy(others, others, s4.at[unit]).wait()
        other_rows = acc.at[which, pl.ds(0, (ROWS - 1) * N1L), lanes]
        pltpu.make_async_copy(other_rows, other_rows, s5.at[unit]).wait()
        out = (oh_ref, ox_ref)[which].at[:, :, lanes]
        pltpu.make_async_copy(out, out, r5.at[unit]).wait()


def hand_over(a_ref, b_ref, c_ref, d_ref, held, in_sem, out_sem):
    pieces = [
        (n, pl.ds(4 * k, 4), source, target)
        for n, (source, target) in enumerate(((a_ref, c_ref), (b_ref, d_ref)))
        for k in range(4)
    ]
    copies = []
    for k, (n, at, source, _) in enumerate(pieces):
        copies.append(pltpu.make_async_copy(source.at[at], held.at[n, at], in_sem.at[k]))
        copies[-1].start()
    back = []
    for k, (n, at, _, target) in enumerate(pieces):
        copies[k].wait()
        back.append(pltpu.make_async_copy(held.at[n, at], target.at[at], out_sem.at[k]))
        back[-1].start()
    for copy in back:
        copy.wait()


def local(grad_out, input_spectrum, filter_spectrum):
    first, last, inner, place = (jnp.asarray(t) for t in tables())
    out = jax.ShapeDtypeStruct((CH, N1L, B), F32)
    dma = pltpu.SemaphoreType.DMA
    results = pl.pallas_call(
        kernel,
        out_shape=(out, out),
        in_specs=[pl.BlockSpec(memory_space=pl.ANY)] * 7,
        out_specs=(pl.BlockSpec(memory_space=pl.ANY),) * 2,
        scratch_shapes=[
            pltpu.VMEM((2, 2, CH, K1L, N2), F32),
            pltpu.VMEM((CH, N1L, B), F32),
            pltpu.VMEM((2, 2, CH, RAD * K1L, B), F32),
            pltpu.VMEM((2, 2 * N1, HALF1), BF16),
            pltpu.VMEM((2, ROWS, HALF1, 128), BF16),
            pltpu.VMEM((4, 2 * B, 2 * B), BF16),
            pltpu.VMEM((B, B), BF16),
            pltpu.VMEM((HALF1, B), F32),
            pltpu.VMEM((2, 2, HALF1, B // 2), BF16),
            pltpu.VMEM((DEVS, 2, K1L, B), F32),
            pltpu.VMEM((DEVS, 2, K1L, B), F32),
            pltpu.VMEM((2, RAD, K1L, B), F32),
            pltpu.VMEM((2, RAD, K1L, B), F32),
            pltpu.VMEM((PER * 64, 2 * B), BF16),
            pltpu.VMEM((PER * 64, 2 * B), BF16),
            pltpu.VMEM((GROUPS, PER * 64, 2 * B), F32),
            pltpu.VMEM((PER * 64, 2 * B), F32),
            pltpu.VMEM((2, DEVS, 2, K1L, B), F32),
            pltpu.VMEM((2, DEVS, 2, K1L, B), F32),
            pltpu.VMEM((2, HALF1, B), F32),
            dma((7,)),
            dma, dma((2,)),
            dma, dma((GROUPS,)),
            dma((len(UNITS),)), dma((len(UNITS), GROUPS)),
            dma((len(UNITS),)), dma((len(UNITS),)),
        ],
        compiler_params=pltpu.CompilerParams(
            collective_id=0, has_side_effects=True, vmem_limit_bytes=56 * 2**20
        ),
    )(grad_out, input_spectrum, filter_spectrum, first, last, inner, place)
    return pl.pallas_call(
        hand_over,
        out_shape=(out, out),
        in_specs=[pl.BlockSpec(memory_space=pl.ANY)] * 2,
        out_specs=(pl.BlockSpec(memory_space=pl.ANY),) * 2,
        scratch_shapes=[pltpu.VMEM((2, CH, N1L, B), F32), dma((8,)), dma((8,))],
    )(*results)


def solution(mesh):
    return jax.shard_map(
        local,
        mesh=mesh,
        in_specs=(
            P(None, "row", "col"),
            P(None, None, ("row", "col"), None),
            P(None, None, ("row", "col"), None),
        ),
        out_specs=(P(None, "row", "col"), P(None, "row", "col")),
        check_vma=False,
    )
```

```python
import functools

import jax
import jax.numpy as jnp
import ml_dtypes
import numpy as np
from jax import lax
from jax.experimental import pallas as pl
from jax.experimental.pallas import tpu as pltpu
from jax.sharding import PartitionSpec as P

MESH = pl.DeviceIdType.MESH
F32 = jnp.float32
BF16 = jnp.bfloat16

ROWS, COLS = 16, 8
DEVS = ROWS * COLS
CH = 16
N1, N2 = 1024, 2048
HALF1 = N1 // 2
TOTAL = N1 * N2
K1L = N1 // DEVS
N1L = HALF1 // ROWS
B = N2 // COLS
RAD = 8
GROUPS, PER = 4, 4
UNITS = ((0, pl.ds(0, B)), (1, pl.ds(0, B)))
HALVES = (pl.ds(0, B // 2), pl.ds(B // 2, B // 2))
ROOT_HALF = float(np.sqrt(0.5))


def split_table(table):
    table = np.asarray(table, np.float64)
    high = table.astype(np.float32).astype(ml_dtypes.bfloat16)
    low = (table - high.astype(np.float64)).astype(np.float32).astype(ml_dtypes.bfloat16)
    return np.stack([high, low])


@functools.lru_cache(None)
def tables():
    n1 = np.arange(HALF1)
    k1 = np.arange(N1)
    angle = 2 * np.pi * ((k1[:, None] * n1[None, :]) % N1) / N1
    first = np.stack([np.cos(angle), -np.sin(angle)]).reshape(2, DEVS, K1L, HALF1)
    first = first.transpose(1, 0, 2, 3).reshape(2 * N1, HALF1)
    last = (first.T / TOTAL).reshape(HALF1, ROWS, 2 * N1 // ROWS).transpose(1, 0, 2)
    b = np.arange(B)
    angle = 2 * np.pi * ((b[:, None] * b[None, :]) % B) / B
    c, s = np.cos(angle), np.sin(angle)
    inner = np.block([[c, -s], [s, c]])
    back = np.block([[c, s], [-s, c]])
    place = np.zeros((B, B))
    place[b, (b % RAD) * (B // RAD) + b // RAD] = 1
    return (
        split_table(first),
        split_table(last),
        np.concatenate([split_table(inner), split_table(back)]),
        place.astype(ml_dtypes.bfloat16),
    )


def split(value):
    high = value.astype(BF16)
    low = (value - high.astype(F32)).astype(BF16)
    return high, low


def mm(a, b):
    return jnp.dot(a, b, preferred_element_type=F32)


def mm3(ah, al, bh, bl):
    return mm(ah, bh) + (mm(ah, bl) + mm(al, bh))


def dft4(re, im, sign):
    p0r, p0i = re[0] + re[2], im[0] + im[2]
    p1r, p1i = re[0] - re[2], im[0] - im[2]
    r0r, r0i = re[1] + re[3], im[1] + im[3]
    r1r, r1i = re[1] - re[3], im[1] - im[3]
    out_r = [p0r + r0r, None, p0r - r0r, None]
    out_i = [p0i + r0i, None, p0i - r0i, None]
    if sign > 0:
        out_r[1], out_i[1] = p1r - r1i, p1i + r1r
        out_r[3], out_i[3] = p1r + r1i, p1i - r1r
    else:
        out_r[1], out_i[1] = p1r + r1i, p1i - r1r
        out_r[3], out_i[3] = p1r - r1i, p1i + r1r
    return out_r, out_i


def dft8(re, im, sign):
    ur = [re[a] + re[a + 4] for a in range(4)]
    ui = [im[a] + im[a + 4] for a in range(4)]
    vr = [re[a] - re[a + 4] for a in range(4)]
    vi = [im[a] - im[a + 4] for a in range(4)]
    even_r, even_i = dft4(ur, ui, sign)
    if sign > 0:
        v1 = ((vr[1] - vi[1]) * ROOT_HALF, (vi[1] + vr[1]) * ROOT_HALF)
        v2 = (-vi[2], vr[2])
        v3 = ((vr[3] + vi[3]) * -ROOT_HALF, (vr[3] - vi[3]) * ROOT_HALF)
    else:
        v1 = ((vr[1] + vi[1]) * ROOT_HALF, (vi[1] - vr[1]) * ROOT_HALF)
        v2 = (vi[2], -vr[2])
        v3 = ((vi[3] - vr[3]) * ROOT_HALF, (vr[3] + vi[3]) * -ROOT_HALF)
    odd_r, odd_i = dft4([vr[0], v1[0], v2[0], v3[0]], [vi[0], v1[1], v2[1], v3[1]], sign)
    out_r = [None] * 8
    out_i = [None] * 8
    for t in range(4):
        out_r[2 * t], out_i[2 * t] = even_r[t], even_i[t]
        out_r[2 * t + 1], out_i[2 * t + 1] = odd_r[t], odd_i[t]
    return out_r, out_i


def row_at(row, q, m, way):
    yl, z, core = lax.div(row, 8), lax.rem(lax.div(row, 2), 4), lax.rem(row, 2)
    dyl, dc, dz = lax.div(m, 2), lax.rem(m, 2), lax.rem(q + m, 4)
    dz = dz if way > 0 else 4 - dz
    return lax.rem(yl + dyl, 2) * 8 + lax.rem(z + dz, 4) * 2 + lax.rem(core + dc, 2)


def col_at(col, i):
    yh, x = lax.div(col, 4), lax.rem(col, 4)
    return lax.rem(yh + lax.div(i, 4), 2) * 4 + lax.rem(x + lax.rem(i, 4), 4)


def loop(lower, upper, body):
    def step(i, carry):
        body(i)
        return carry

    lax.fori_loop(lower, upper, step, 0)


def spread(row, col, q, way, send):
    turn = row + col + lax.div(row, 4)
    rows = [row_at(row, q, lax.rem(m + turn, PER), way) for m in range(PER)]
    step = 2 * lax.rem(row, 4) + 1
    start = row * 3 + col * 5 + lax.div(row, 4)

    def visit(i):
        base = i * step + start
        for m, r in enumerate(rows):
            c = lax.rem(base + 3 * m, COLS)
            pl.when((r != row) | (c != col))(functools.partial(send, r, c))

    loop(0, COLS, visit)


def kernel(
    grad_ref, sx_ref, sh_ref, first_ref, last_ref, inner_ref, place_ref,
    oh_ref, ox_ref,
    raw, xin, spec, first, last, inner, place, xg, xs, bsend, brecv, va, vt,
    ah, al, us, vs, tsend, trecv, acc,
    lsem, s1, r1, s2, r2, s4, r4, s5, r5,
):
    row = lax.axis_index("row")
    col = lax.axis_index("col")
    me = row * COLS + col

    barrier = pltpu.get_barrier_semaphore()

    def greet(i):
        r = row + i
        r = jnp.where(r >= ROWS, r - ROWS, r)
        for j in range(COLS):
            c = col + j
            c = jnp.where(c >= COLS, c - COLS, c)
            pl.semaphore_signal(barrier, inc=1, device_id=(r, c), device_id_type=MESH)

    for j in range(1, COLS):
        c = col + j
        c = jnp.where(c >= COLS, c - COLS, c)
        pl.semaphore_signal(barrier, inc=1, device_id=(row, c), device_id_type=MESH)
    loop(1, ROWS, greet)

    load_x = pltpu.make_async_copy(grad_ref, xin, lsem.at[6])
    load_x.start()
    loads = [
        pltpu.make_async_copy(sh_ref, raw.at[0], lsem.at[0]),
        pltpu.make_async_copy(sx_ref, raw.at[1], lsem.at[1]),
        pltpu.make_async_copy(place_ref, place, lsem.at[2]),
        pltpu.make_async_copy(first_ref, first, lsem.at[3]),
        pltpu.make_async_copy(inner_ref, inner, lsem.at[4]),
        pltpu.make_async_copy(last_ref, last, lsem.at[5]),
    ]
    for n in (3, 0, 1, 2, 4, 5):
        loads[n].start()

    k1 = me * K1L + lax.broadcasted_iota(jnp.int32, (K1L, B), 0)
    lane = lax.broadcasted_iota(jnp.int32, (K1L, B), 1)

    def turn(a):
        phase = lax.rem(k1 * a, TOTAL // B)
        phase = jnp.where(phase > TOTAL // B // 2, phase - TOTAL // B, phase)
        angle = phase.astype(F32) * (2.0 * np.pi * B / TOTAL)
        va[0, a] = jnp.cos(angle)
        va[1, a] = jnp.sin(angle)
        phase = lane * (k1 + N1 * a)
        phase = jnp.where(phase > TOTAL // 2, phase - TOTAL, phase)
        angle = phase.astype(F32) * (2.0 * np.pi / TOTAL)
        vt[0, a] = jnp.cos(angle)
        vt[1, a] = jnp.sin(angle)

    pl.semaphore_wait(barrier, DEVS - 1)

    own_rows = pl.ds(pl.multiple_of(row * N1L, N1L), N1L)
    load_x.wait()
    for h, lanes in enumerate(HALVES):
        pltpu.make_async_copy(xin.at[row, :, lanes], xg.at[own_rows, lanes], r1.at[h]).start()

        def send_x(n):
            r = 2 * lax.rem(lax.div(row, 2) + lax.rem(n, ROWS // 2), ROWS // 2) + lax.div(n, ROWS // 2)

            @pl.when(r != row)
            def _():
                pltpu.make_async_remote_copy(
                    src_ref=xin.at[r, :, lanes], dst_ref=xg.at[own_rows, lanes], send_sem=s1,
                    recv_sem=r1.at[h], device_id=(r, col), device_id_type=MESH,
                ).start()

        loop(0, ROWS, send_x)

    lane128 = lax.broadcasted_iota(jnp.int32, (16, 128), 1)

    def order(n):
        which, part, c0 = lax.div(n, 8), lax.rem(lax.div(n, 4), 2), lax.rem(n, 4) * 4
        blocks = []
        for c in range(4):
            whole = raw[which, part, c0 + c]
            blocks += [whole[:, j * B : (j + 1) * B] for j in range(RAD)]
        high, low = split(jnp.concatenate(blocks, axis=0))
        placed = mm(high, place[...]) + mm(low, place[...])
        for c in range(4):
            for h in range(2):
                runs = []
                for i in range(4):
                    at = c * 64 + i * 8
                    runs.append(
                        jnp.concatenate(
                            [
                                placed[at : at + 8, h * 128 : h * 128 + 128],
                                placed[at + 32 : at + 40, h * 128 : h * 128 + 128],
                            ],
                            axis=0,
                        )
                    )
                for tt in range(4):
                    t = 4 * h + tt
                    total = None
                    for i in range(4):
                        shift = (32 * (i - tt)) % 128
                        moved = pltpu.roll(runs[i], shift, 1) if shift else runs[i]
                        if total is None:
                            total = moved
                        else:
                            total = jnp.where(lane128 >= 32 * i, moved, total)
                    spec[which, part, c0 + c, t * 8 : t * 8 + 8, 0:128] = total[0:8]
                    spec[which, part, c0 + c, t * 8 : t * 8 + 8, 128:256] = total[8:16]


    loads[3].wait()
    for h, lanes in enumerate(HALVES):
        arrived = xg.at[:, lanes]
        pltpu.make_async_copy(arrived, arrived, r1.at[h]).wait()
        high, low = split(xg[:, lanes])
        xs[0, h] = high
        xs[1, h] = low

        def first_group(q):
            rows = [row_at(row, q, m, 1) for m in range(PER)]
            at = [pl.ds(pl.multiple_of(r * 128, 128), 128) for r in rows]
            wh = jnp.concatenate([first[0, a] for a in at], axis=0)
            wl = jnp.concatenate([first[1, a] for a in at], axis=0)
            value = mm3(wh, wl, xs[0, h], xs[1, h])
            for m in range(PER):
                block = value[m * 128 : (m + 1) * 128].reshape(COLS, 2, K1L, B // 2)
                bsend[pl.ds(rows[m] * COLS, COLS), :, :, lanes] = block

            @pl.when(q == 0)
            def _():
                pltpu.make_async_copy(
                    bsend.at[me, :, :, lanes], brecv.at[me, :, :, lanes], r2.at[q]
                ).start()

            def send(r, c):
                pltpu.make_async_remote_copy(
                    src_ref=bsend.at[r * COLS + c, :, :, lanes], dst_ref=brecv.at[me, :, :, lanes],
                    send_sem=s2, recv_sem=r2.at[q], device_id=(r, c), device_id_type=MESH,
                ).start()

            spread(row, col, q, 1, send)

        loop(0, GROUPS, first_group)

    loop(0, RAD, turn)
    for load in loads[:3]:
        load.wait()
    loop(0, 16, order)
    loads[4].wait()

    def send_back(unit, q):
        which, lanes = UNITS[unit]

        @pl.when(q == 0)
        def _():
            pltpu.make_async_copy(
                tsend.at[which, me, :, :, lanes], trecv.at[which, me, :, :, lanes], r4.at[unit, q]
            ).start()

        def send(r, c):
            pltpu.make_async_remote_copy(
                src_ref=tsend.at[which, r * COLS + c, :, :, lanes],
                dst_ref=trecv.at[which, me, :, :, lanes],
                send_sem=s4.at[unit], recv_sem=r4.at[unit, q], device_id=(r, c),
                device_id_type=MESH,
            ).start()

        spread(row, col, q, -1, send)

    def inverse(which, q):
        def product(m):
            c = row_at(row, q, m, -1)
            at = pl.ds(pl.multiple_of(m * 64, 64), 64)
            ur, ui = us[q, at, 0:B], us[q, at, B : 2 * B]
            sr, si = spec[which, 0, c], spec[which, 1, c]
            high, low = split(ur * sr + ui * si)
            ah[at, 0:B] = high
            al[at, 0:B] = low
            high, low = split(ui * sr - ur * si)
            ah[at, B : 2 * B] = high
            al[at, B : 2 * B] = low

        loop(0, PER, product)
        vs[...] = mm3(ah[...], al[...], inner[2], inner[3])

        def turn_back(m):
            c = row_at(row, q, m, -1)
            re, im = [], []
            for t in range(RAD):
                at = pl.ds(pl.multiple_of(m * 64 + t * 8, 8), 8)
                r, i = vs[at, 0:B], vs[at, B : 2 * B]
                cs, sn = vt[0, t], vt[1, t]
                re.append(r * cs - i * sn)
                im.append(i * cs + r * sn)
            re, im = dft8(re, im, 1)
            for a in range(RAD):
                r, i = re[a], im[a]
                if a:
                    cs, sn = va[0, a], va[1, a]
                    r, i = r * cs - i * sn, i * cs + r * sn
                tsend[which, c * COLS + a, 0] = r
                tsend[which, c * COLS + a, 1] = i

        loop(0, PER, turn_back)


    def forward(q):
        group = brecv.at[pl.ds(0, PER * COLS)]
        pltpu.make_async_copy(group, group, r2.at[q]).wait()

        def outer(m):
            c = row_at(row, q, m, -1)
            re, im = [], []
            for a in range(RAD):
                r, i = brecv[c * COLS + a, 0], brecv[c * COLS + a, 1]
                if a:
                    cs, sn = va[0, a], va[1, a]
                    r, i = r * cs + i * sn, i * cs - r * sn
                re.append(r)
                im.append(i)
            re, im = dft8(re, im, -1)
            out_r, out_i = [], []
            for t in range(RAD):
                cs, sn = vt[0, t], vt[1, t]
                out_r.append(re[t] * cs + im[t] * sn)
                out_i.append(im[t] * cs - re[t] * sn)
            at = pl.ds(pl.multiple_of(m * 64, 64), 64)
            high, low = split(jnp.concatenate(out_r, axis=0))
            ah[at, 0:B] = high
            al[at, 0:B] = low
            high, low = split(jnp.concatenate(out_i, axis=0))
            ah[at, B : 2 * B] = high
            al[at, B : 2 * B] = low

        loop(0, PER, outer)
        us[q] = mm3(ah[...], al[...], inner[0], inner[1])
        inverse(0, q)
        send_back(0, q)

    def second(q):
        inverse(1, q)
        send_back(1, q)

    loop(0, GROUPS, forward)
    loop(0, GROUPS, second)

    loads[5].wait()

    for unit, (which, lanes) in enumerate(UNITS):
        out = (oh_ref, ox_ref)[which]

        def gathered(q):
            group = trecv.at[which, pl.ds(0, PER * COLS), :, :, lanes]
            pltpu.make_async_copy(group, group, r4.at[unit, q]).wait()
            rows = [row_at(row, q, m, 1) for m in range(PER)]
            parts = [trecv[which, pl.ds(r * COLS, COLS), :, :, lanes] for r in rows]
            whole = jnp.concatenate([p.reshape(128, p.shape[-1]) for p in parts], axis=0)
            return rows, *split(whole)

        def added(rows, at, high, low):
            wh = jnp.concatenate([last[0, r, at] for r in rows], axis=1)
            wl = jnp.concatenate([last[1, r, at] for r in rows], axis=1)
            return mm3(wh, wl, high, low)

        def last_group(q):
            rows, high, low = gathered(q)
            value = added(rows, pl.ds(0, HALF1), high, low)

            @pl.when(q == 0)
            def _():
                acc[which, :, lanes] = value

            @pl.when(q > 0)
            def _():
                acc[which, :, lanes] += value

        loop(0, GROUPS - 1, last_group)

        rows, high, low = gathered(GROUPS - 1)

        def finish(k):
            half = lax.rem(lax.div(row, ROWS // 2) + k, 2)
            at = pl.ds(pl.multiple_of(half * (HALF1 // 2), HALF1 // 2), HALF1 // 2)
            acc[which, at, lanes] += added(rows, at, high, low)

            @pl.when(k == 0)
            def _():
                pltpu.make_async_copy(
                    acc.at[which, own_rows, lanes], out.at[row, :, lanes], r5.at[unit]
                ).start()

            def send_out(i):
                r = half * (ROWS // 2) + lax.rem(row + i, ROWS // 2)
                pltpu.make_async_remote_copy(
                    src_ref=acc.at[which, pl.ds(pl.multiple_of(r * N1L, N1L), N1L), lanes],
                    dst_ref=out.at[row, :, lanes], send_sem=s5.at[unit], recv_sem=r5.at[unit],
                    device_id=(r, col), device_id_type=MESH,
                ).start()

            loop(jnp.where(k == 0, 1, 0), ROWS // 2, send_out)

        loop(0, 2, finish)

    other_rows = xg.at[pl.ds(0, (ROWS - 1) * N1L)]
    pltpu.make_async_copy(other_rows, other_rows, s1).wait()
    others = bsend.at[pl.ds(0, DEVS - 1)]
    pltpu.make_async_copy(others, others, s2).wait()
    for unit, (which, lanes) in enumerate(UNITS):
        others = tsend.at[which, pl.ds(0, DEVS - 1), :, :, lanes]
        pltpu.make_async_copy(others, others, s4.at[unit]).wait()
        other_rows = acc.at[which, pl.ds(0, (ROWS - 1) * N1L), lanes]
        pltpu.make_async_copy(other_rows, other_rows, s5.at[unit]).wait()
        out = (oh_ref, ox_ref)[which].at[:, :, lanes]
        pltpu.make_async_copy(out, out, r5.at[unit]).wait()


def hand_over(a_ref, b_ref, c_ref, d_ref, held, in_sem, out_sem):
    pieces = [
        (n, pl.ds(4 * k, 4), source, target)
        for n, (source, target) in enumerate(((a_ref, c_ref), (b_ref, d_ref)))
        for k in range(4)
    ]
    copies = []
    for k, (n, at, source, _) in enumerate(pieces):
        copies.append(pltpu.make_async_copy(source.at[at], held.at[n, at], in_sem.at[k]))
        copies[-1].start()
    back = []
    for k, (n, at, _, target) in enumerate(pieces):
        copies[k].wait()
        back.append(pltpu.make_async_copy(held.at[n, at], target.at[at], out_sem.at[k]))
        back[-1].start()
    for copy in back:
        copy.wait()


def local(grad_out, input_spectrum, filter_spectrum):
    first, last, inner, place = (jnp.asarray(t) for t in tables())
    out = jax.ShapeDtypeStruct((CH, N1L, B), F32)
    dma = pltpu.SemaphoreType.DMA
    results = pl.pallas_call(
        kernel,
        out_shape=(out, out),
        in_specs=[pl.BlockSpec(memory_space=pl.ANY)] * 7,
        out_specs=(pl.BlockSpec(memory_space=pl.ANY),) * 2,
        scratch_shapes=[
            pltpu.VMEM((2, 2, CH, K1L, N2), F32),
            pltpu.VMEM((CH, N1L, B), F32),
            pltpu.VMEM((2, 2, CH, RAD * K1L, B), F32),
            pltpu.VMEM((2, 2 * N1, HALF1), BF16),
            pltpu.VMEM((2, ROWS, HALF1, 128), BF16),
            pltpu.VMEM((4, 2 * B, 2 * B), BF16),
            pltpu.VMEM((B, B), BF16),
            pltpu.VMEM((HALF1, B), F32),
            pltpu.VMEM((2, 2, HALF1, B // 2), BF16),
            pltpu.VMEM((DEVS, 2, K1L, B), F32),
            pltpu.VMEM((DEVS, 2, K1L, B), F32),
            pltpu.VMEM((2, RAD, K1L, B), F32),
            pltpu.VMEM((2, RAD, K1L, B), F32),
            pltpu.VMEM((PER * 64, 2 * B), BF16),
            pltpu.VMEM((PER * 64, 2 * B), BF16),
            pltpu.VMEM((GROUPS, PER * 64, 2 * B), F32),
            pltpu.VMEM((PER * 64, 2 * B), F32),
            pltpu.VMEM((2, DEVS, 2, K1L, B), F32),
            pltpu.VMEM((2, DEVS, 2, K1L, B), F32),
            pltpu.VMEM((2, HALF1, B), F32),
            dma((7,)),
            dma, dma((2,)),
            dma, dma((GROUPS,)),
            dma((len(UNITS),)), dma((len(UNITS), GROUPS)),
            dma((len(UNITS),)), dma((len(UNITS),)),
        ],
        compiler_params=pltpu.CompilerParams(
            collective_id=0, has_side_effects=True, vmem_limit_bytes=56 * 2**20
        ),
    )(grad_out, input_spectrum, filter_spectrum, first, last, inner, place)
    return pl.pallas_call(
        hand_over,
        out_shape=(out, out),
        in_specs=[pl.BlockSpec(memory_space=pl.ANY)] * 2,
        out_specs=(pl.BlockSpec(memory_space=pl.ANY),) * 2,
        scratch_shapes=[pltpu.VMEM((2, CH, N1L, B), F32), dma((8,)), dma((8,))],
    )(*results)


def solution(mesh):
    return jax.shard_map(
        local,
        mesh=mesh,
        in_specs=(
            P(None, "row", "col"),
            P(None, None, ("row", "col"), None),
            P(None, None, ("row", "col"), None),
        ),
        out_specs=(P(None, "row", "col"), P(None, "row", "col")),
        check_vma=False,
    )
```
